256 devices in a mesh: dp: 8 (over y, core), et: 32 (over z, x).
Axes of the slice: x: 4, y: 4, z: 8, core: 2. Of those that a mesh axis runs over, the one named last changes fastest.
Arguments:
- tokens: bfloat16 [1024, 4096], P('dp'), may hold values from -6 to 6
- routed_experts: int32 [1024, 2], P('dp'), may hold values from 0 to 7, all different within a row; in each aligned block of 128 rows (0 to 127, 128 to 255, ...) at most 64 rows name the same one
- choice_weights: float32 [1024, 2], P('dp'), may hold values from 0.1 to 0.9
- gate_up_weight: bfloat16 [2, 4096, 86016], P(None, None, ('et', 'dp')), may hold values from -0.09375 to 0.09375
- down_weight: bfloat16 [86016, 4096], P(('et', 'dp')), may hold values from -0.0625 to 0.0625
- adapter_first_factors: bfloat16 [2, 4096, 512], P(None, 'dp'), may hold values from -0.09375 to 0.09375
- adapter_second_factors: bfloat16 [2, 64, 86016], P(None, None, ('et', 'dp')), may hold values from -0.75 to 0.75
- cotangent: bfloat16 [1024, 4096], P('dp'), may hold values from -6 to 6
Outputs:
- mixed: bfloat16 [1024, 4096], P('dp', 'et')
- token_gradient: bfloat16 [1024, 4096], P('dp', 'et')
- first_factors_gradient: float32 [2, 4096, 512], P(None, 'dp', 'et')
- second_factors_gradient: float32 [2, 64, 86016], P(None, None, ('et', 'dp'))
The draws below stay inside these ranges and needn't reach their ends.
Inputs may be any that keep to these rules, and one draw needn't show every extreme that they name: `routed_experts`: each token names two different experts. Within the tokens of one index of dp (aligned blocks of 128 rows) no expert is named by more than 64 tokens, and in some block one expert is named by exactly 64.
All inputs are finite; a program needn't handle non-finite values.
Results may differ from the reference program's by a relative error of at most 0.024.
Values may be sent and summed in bfloat16 or wider, within the bound.
No kernel may reach another device: no remote copies, remote signals or barrier semaphores. Data moves between devices by JAX's collectives and lax.ppermute only.
A program may use at most 128 MiB of HBM per device.

```python
import math
import jax
import jax.numpy as jnp
import numpy as np
from jax import lax

MODEL_DIM = 4096
EXPERT_COUNT = 8
HIDDEN_KEPT = 10752
ADAPTER_RANK = 64
TOK_DEV = 128
CAP = 64
TOKENS = 1024
SUB = 4
FF_DEV = 336
ROWS = 512
ALL_HIDDEN = 86016
ALL_ADAPTER_COLS = 512
N_DP = 8


def block_levels(stream_key, extent, pieces, smallest, high):
    def one(dim, blocks):
        steps = jax.random.uniform(jax.random.fold_in(jax.random.fold_in(stream_key, 6), dim), (blocks,), jnp.float32, smallest / len(pieces), high / len(pieces))
        return jnp.repeat(jnp.exp(steps), extent[dim] // blocks).reshape((-1,) + (1,) * (len(extent) - dim - 1))

    factor_of = one(*pieces[0])
    for cut in pieces[1:]:
        factor_of = factor_of * one(*cut)
    return factor_of


def routed_block(own_key, own, number, rows, count, top, bound, slope):
    order = jax.random.permutation(own_key, count)
    crowded, common = load_shares(count, rows * top, bound, slope, True), load_shares(count, rows * top, bound, slope, False)
    places = jnp.arange(count)

    def named(sizes, offset_by):
        used = int((sizes > 0).sum())
        fixed = max(1, used // 4)
        shifted = fixed + (places - fixed + offset_by * (used - fixed)) % max(1, count - fixed)
        return jnp.zeros((count,), jnp.int32).at[order[jnp.where(places < fixed, places, shifted)]].set(jnp.asarray(sizes, jnp.int32))

    sizes = jnp.where(number % 4 == 0, named(crowded, number // 4), named(common, number - number // 4 - 1))
    mixed = jax.random.permutation(jax.random.fold_in(own, 3), count)
    source_of, receiver = mixed[0:count // 2 * 2:2], mixed[1:count // 2 * 2:2]
    slack = jnp.minimum(sizes[source_of] - 1, bound - sizes[receiver]) // 2
    slack = jnp.where((source_of == order[0]) | (receiver == order[0]) | (sizes[receiver] == 0), 0, jnp.maximum(slack, 0))
    shifted = jax.random.randint(jax.random.fold_in(own, 4), (count // 2,), 0, 1 << 20) % (slack + 1)
    sizes = sizes.at[source_of].add(-shifted).at[receiver].add(shifted)
    labels = jnp.searchsorted(jnp.cumsum(sizes), jnp.arange(rows * top), side="right").astype(jnp.int32)
    listing = labels.reshape(top, rows).T
    listing = listing[jax.random.permutation(jax.random.fold_in(own, 1), rows)]
    offset_by = jax.random.randint(jax.random.fold_in(own, 2), (rows, 1), 0, top)
    return jnp.take_along_axis(listing, (jnp.arange(top)[None, :] + offset_by) % top, axis=1)


def load_shares(count, total, limit, skew, full):
    loads = [(1 << 20) // math.isqrt(rank ** skew) + 1 for rank in range(1, count + 1)]
    largest = limit if full else min(limit, max(-(-total // count), total * loads[0] // sum(loads)))
    least = 1 if total - largest >= count - 1 else 0
    holding, rest = [largest] + [least] * (count - 1), total - largest - least * (count - 1)
    while rest > 0:
        movable = [i for i in range(1, count) if holding[i] < largest] or [i for i in range(1, count) if holding[i] < limit]
        whole, remaining = sum([loads[i] for i in movable]), rest
        for i in movable:
            more = min(limit - holding[i], max(1, remaining * loads[i] // whole), rest)
            holding[i] = holding[i] + more
            rest = rest - more
    return np.array(holding)


def gaussian(key, shape, deviation, limit, cuts=(), kind=jnp.bfloat16):
    drawn = deviation * jax.random.normal(key, shape, jnp.float32)
    if cuts:
        drawn = drawn * block_levels(key, shape, cuts, -0.22, 0.18)
    return jnp.clip(drawn, -limit, limit).astype(kind)


def setup_inputs(seed: int = 0) -> dict:
    keys = jax.random.split(jax.random.key(seed), 9)
    tokens = gaussian(keys[0], (TOKENS, MODEL_DIM), 1.0, 6.0, ((0, 8),))
    routed_experts_keys = jax.random.split(jax.random.fold_in(keys[1], 1), TOKENS // TOK_DEV)
    routed_experts_turns = jax.random.permutation(jax.random.fold_in(keys[1], 3), TOKENS // TOK_DEV)
    routed_experts = jax.vmap(lambda own, number: routed_block(jax.random.fold_in(keys[1], 2), own, number, TOK_DEV, EXPERT_COUNT, 2, CAP, 2))(routed_experts_keys, routed_experts_turns).reshape((TOKENS, 2))
    choice_weights = jnp.clip(0.1 + 0.79999997 * jax.random.uniform(keys[2], (TOKENS, 2), jnp.float32) ** block_levels(keys[2], (TOKENS, 2), ((0, 8),), -0.2, 0.2), 0.1, 0.9)
    gate_up_weight = gaussian(keys[3], (2, MODEL_DIM, ALL_HIDDEN), MODEL_DIM ** -0.5, 0.09375, ((2, 256),))
    down_weight = gaussian(keys[4], (ALL_HIDDEN, MODEL_DIM), HIDDEN_KEPT ** -0.5, 0.0625, ((0, 256),))
    adapter_first_factors = gaussian(keys[5], (2, MODEL_DIM, ALL_ADAPTER_COLS), MODEL_DIM ** -0.5, 0.09375, ((1, 8),))
    adapter_second_factors = gaussian(keys[6], (2, ADAPTER_RANK, ALL_HIDDEN), ADAPTER_RANK ** -0.5, 0.75, ((2, 256),))
    cotangent = gaussian(keys[7], (TOKENS, MODEL_DIM), 1.0, 6.0, ((0, 8),))
    return dict(tokens=tokens, routed_experts=routed_experts, choice_weights=choice_weights, gate_up_weight=gate_up_weight, down_weight=down_weight, adapter_first_factors=adapter_first_factors, adapter_second_factors=adapter_second_factors, cotangent=cotangent)


ADAPTER_SCALE = 0.5


def rounded(values):
    return lax.optimization_barrier(values.astype(jnp.bfloat16)).astype(jnp.float32)


def route_tables(routed_experts, choice_weights):
    route_ids = routed_experts.reshape(N_DP, TOK_DEV, 2)
    gate_values = choice_weights.reshape(N_DP, TOK_DEV, 2)
    experts = jnp.arange(EXPERT_COUNT, dtype=jnp.int32)
    named_hits = route_ids[:, :, :, None] == experts
    chosen = jnp.sum(named_hits.astype(jnp.int32), axis=2).astype(jnp.int32)
    weight = jnp.sum(jnp.where(named_hits, gate_values[:, :, :, None], 0.0), axis=2)
    placed = (jnp.cumsum(chosen, axis=1) - chosen).astype(jnp.int32)
    return chosen, weight, placed


def split_blocks(values):
    return values.reshape(values.shape[0], SUB * N_DP, FF_DEV).transpose(1, 0, 2)


def reference(tokens, routed_experts, choice_weights, gate_up_weight, down_weight, adapter_first_factors, adapter_second_factors, cotangent):
    chosen, weight, placed = route_tables(routed_experts, choice_weights)
    slot_ids = jnp.arange(CAP, dtype=jnp.int32)
    slot_match = (chosen[:, :, :, None] == 1) & (placed[:, :, :, None] == slot_ids)
    positions = jnp.arange(TOK_DEV, dtype=jnp.int32)
    row_token = jnp.sum(jnp.where(slot_match, positions[None, :, None, None], 0), axis=1).astype(jnp.int32)
    row_valid = jnp.any(slot_match, axis=1)
    row_gate = jnp.sum(jnp.where(slot_match, weight[:, :, :, None], 0.0), axis=1)
    block_base = jnp.arange(N_DP, dtype=jnp.int32) * TOK_DEV
    flat_index = (row_token + block_base[:, None, None]).astype(jnp.int32)
    rows_x = jnp.where(row_valid[..., None], tokens[flat_index], jnp.zeros((), tokens.dtype))
    scaled_dy = (cotangent[flat_index].astype(jnp.float32) * row_gate[..., None]).astype(jnp.bfloat16)
    rows_dy = jnp.where(row_valid[..., None], scaled_dy, jnp.zeros((), scaled_dy.dtype))
    rows_x = rows_x.transpose(1, 0, 2, 3).reshape(EXPERT_COUNT, ROWS, MODEL_DIM)
    rows_dy = rows_dy.transpose(1, 0, 2, 3).reshape(EXPERT_COUNT, ROWS, MODEL_DIM)
    row_base = jnp.arange(N_DP, dtype=jnp.int32) * CAP
    token_row = (placed + row_base[:, None, None]).reshape(TOKENS, EXPERT_COUNT).astype(jnp.int32)
    token_row = jnp.minimum(token_row, ROWS - 1)
    token_hit = chosen.reshape(TOKENS, EXPERT_COUNT) == 1
    token_weight = weight.reshape(TOKENS, EXPERT_COUNT)

    def expert_pass(operands):
        expert_position, expert_rows, expert_grads = operands
        gate_up = lax.dynamic_slice_in_dim(gate_up_weight, expert_position * HIDDEN_KEPT, HIDDEN_KEPT, 2)
        down_rows = lax.dynamic_slice_in_dim(down_weight, expert_position * HIDDEN_KEPT, HIDDEN_KEPT, 0)
        first_adapter = lax.dynamic_slice_in_dim(adapter_first_factors, expert_position * ADAPTER_RANK, ADAPTER_RANK, 2)
        second_adapter = lax.dynamic_slice_in_dim(adapter_second_factors, expert_position * HIDDEN_KEPT, HIDDEN_KEPT, 2)
        adapter_cat = jnp.concatenate([first_adapter[0], first_adapter[1]], axis=1)
        reduced_rows = jnp.dot(expert_rows, adapter_cat, preferred_element_type=jnp.float32).astype(jnp.bfloat16)
        gate_preactivation = jnp.dot(expert_rows, gate_up[0], preferred_element_type=jnp.float32)
        gate_preactivation = gate_preactivation + ADAPTER_SCALE * jnp.dot(reduced_rows[:, :ADAPTER_RANK], second_adapter[0], preferred_element_type=jnp.float32)
        up_preactivation = jnp.dot(expert_rows, gate_up[1], preferred_element_type=jnp.float32)
        up_preactivation = up_preactivation + ADAPTER_SCALE * jnp.dot(reduced_rows[:, ADAPTER_RANK:], second_adapter[1], preferred_element_type=jnp.float32)
        hidden = (jax.nn.silu(gate_preactivation) * up_preactivation).astype(jnp.bfloat16)
        down_blocks = down_rows.reshape(SUB * N_DP, FF_DEV, MODEL_DIM)

        def down_block(pair):
            return jnp.dot(pair[0], pair[1], preferred_element_type=jnp.float32).astype(jnp.bfloat16)

        out_blocks = lax.optimization_barrier(lax.map(down_block, (split_blocks(hidden), down_blocks)))
        out_part = jnp.sum(out_blocks.astype(jnp.float32).reshape(SUB, N_DP, ROWS, MODEL_DIM), axis=1)

        grad_hidden = jnp.dot(expert_grads, down_rows.T, preferred_element_type=jnp.float32)
        sigmoid_gate = jax.nn.sigmoid(gate_preactivation)
        grad_gate = (grad_hidden * up_preactivation * sigmoid_gate * (1.0 + gate_preactivation * (1.0 - sigmoid_gate))).astype(jnp.bfloat16)
        grad_up = (grad_hidden * gate_preactivation * sigmoid_gate).astype(jnp.bfloat16)
        second_factor_gradient = ADAPTER_SCALE * jnp.stack([
            jnp.dot(reduced_rows[:, :ADAPTER_RANK].T, grad_gate, preferred_element_type=jnp.float32),
            jnp.dot(reduced_rows[:, ADAPTER_RANK:].T, grad_up, preferred_element_type=jnp.float32)])

        def back_block(parts):
            gate_block_slice, up_block_slice, gate_factor_slice, up_factor_slice, weight_gate, weight_up = parts
            reduced_gate = ADAPTER_SCALE * jnp.dot(gate_block_slice, gate_factor_slice.T, preferred_element_type=jnp.float32)
            reduced_up = ADAPTER_SCALE * jnp.dot(up_block_slice, up_factor_slice.T, preferred_element_type=jnp.float32)
            back_term = jnp.dot(gate_block_slice, weight_gate.T, preferred_element_type=jnp.float32)
            back_term = back_term + jnp.dot(up_block_slice, weight_up.T, preferred_element_type=jnp.float32)
            back_term = back_term + jnp.dot(reduced_gate.astype(jnp.bfloat16), first_adapter[0].T, preferred_element_type=jnp.float32)
            back_term = back_term + jnp.dot(reduced_up.astype(jnp.bfloat16), first_adapter[1].T, preferred_element_type=jnp.float32)
            return back_term.astype(jnp.bfloat16), jnp.concatenate([reduced_gate, reduced_up], axis=1)

        in_blocks, low_blocks = lax.map(back_block, (
            split_blocks(grad_gate), split_blocks(grad_up),
            split_blocks(second_adapter[0]), split_blocks(second_adapter[1]),
            split_blocks(gate_up[0]), split_blocks(gate_up[1])))
        in_blocks = lax.optimization_barrier(in_blocks)
        in_part = jnp.sum(in_blocks.astype(jnp.float32).reshape(SUB, N_DP, ROWS, MODEL_DIM), axis=1)
        reduced_gradient = jnp.sum(low_blocks, axis=0).astype(jnp.bfloat16)
        grad_a = jnp.dot(expert_rows.T, reduced_gradient, preferred_element_type=jnp.float32)
        grad_a = jnp.stack([grad_a[:, :ADAPTER_RANK], grad_a[:, ADAPTER_RANK:]])

        hit_here = lax.dynamic_index_in_dim(token_hit, expert_position, 1, keepdims=False)
        row_here = lax.dynamic_index_in_dim(token_row, expert_position, 1, keepdims=False)
        gate_here = lax.dynamic_index_in_dim(token_weight, expert_position, 1, keepdims=False)
        mixed_terms = rounded(gate_here[None, :, None] * out_part[:, row_here, :])
        mixed_part = jnp.where(hit_here[:, None], jnp.sum(mixed_terms, axis=0), 0.0)
        input_terms = rounded(in_part[:, row_here, :])
        input_part = jnp.where(hit_here[:, None], jnp.sum(input_terms, axis=0), 0.0)
        return mixed_part, input_part, grad_a, second_factor_gradient

    experts = jnp.arange(EXPERT_COUNT, dtype=jnp.int32)
    mixed_parts, input_parts, first_gradients, second_gradients = lax.map(expert_pass, (experts, rows_x, rows_dy))
    mixed = jnp.sum(mixed_parts, axis=0).astype(jnp.bfloat16)
    token_gradient = jnp.sum(input_parts, axis=0).astype(jnp.bfloat16)
    first_factors_gradient = first_gradients.transpose(1, 2, 0, 3).reshape(2, MODEL_DIM, EXPERT_COUNT * ADAPTER_RANK)
    second_factors_gradient = second_gradients.transpose(1, 2, 0, 3).reshape(2, ADAPTER_RANK, EXPERT_COUNT * HIDDEN_KEPT)
    return (mixed, token_gradient, first_factors_gradient, second_factors_gradient)
```

```python
import functools

import jax
import jax.numpy as jnp
from jax import lax
from jax.experimental import pallas as pl
from jax.experimental.pallas import tpu as pltpu
from jax.sharding import Mesh, PartitionSpec as P

ADAPTER_SCALE = 0.5
BF = jnp.bfloat16
F32 = jnp.float32


def shift(values, axis, step):
    n = lax.axis_size(axis)
    return lax.ppermute(values, axis, [(i, (i + step) % n) for i in range(n)])


def crossed(values, step, first):
    n_y, n_c, n_x = lax.axis_size("y"), lax.axis_size("core"), lax.axis_size("x")
    pairs = []
    for y in range(n_y):
        for c in range(n_c):
            for x in range(n_x):
                to = ((y + step) % n_y, x) if c == first else (y, (x + step) % n_x)
                pairs.append(((y * n_c + c) * n_x + x, (to[0] * n_c + c) * n_x + to[1]))
    return lax.ppermute(values, ("y", "core", "x"), pairs)


def gather_rows(own):
    half = own.shape[0] // 2
    behind = shift(own, "y", 1)
    ahead = shift(own, "y", -1)
    own_s = shift(own, "core", 1)
    far_a = shift(behind[:half], "y", 1)
    far_b = shift(ahead[half:], "y", -1)
    ahead_s = shift(ahead, "core", 1)
    behind_s = shift(behind, "core", 1)
    far = jnp.concatenate([far_a, far_b], axis=0)
    far_s = shift(far, "core", 1)
    return jnp.concatenate([own, ahead, far, behind, own_s, ahead_s, far_s, behind_s], axis=0)


def pack_kernel(n, cap, n_z, place, own, came, *outs):
    core, x = place[0], place[1]
    lanes = own.shape[1] // (n_z * n)

    def block(i, q, z):
        start = pl.multiple_of(z * n * lanes + lax.rem(x + q, n) * lanes, lanes)
        rows = pl.ds(i * cap, cap)
        both = own[rows, pl.ds(start, lanes)].astype(F32) + came[rows, pl.ds(start, lanes)].astype(F32)
        return both.astype(BF)

    @pl.when(core == 0)
    def _():
        for i in range(n):
            for q in range(n):
                for z in range(n_z):
                    outs[i][pl.ds(q * cap, cap), pl.ds(z * lanes, lanes)] = block(i, q, z)

    @pl.when(core == 1)
    def _():
        for i in range(n):
            for q in range(n):
                for z in range(n_z):
                    outs[q][pl.ds(i * cap, cap), pl.ds(z * lanes, lanes)] = block(i, q, z)


def add_and_pack(own, came):
    n, n_z = lax.axis_size("y"), lax.axis_size("z")
    cap = own.shape[0] // n
    width = own.shape[1] // n
    place = jnp.stack([lax.axis_index("core"), lax.axis_index("x")]).astype(jnp.int32)
    vmem = pl.BlockSpec(memory_space=pltpu.VMEM)
    return pl.pallas_call(
        functools.partial(pack_kernel, n, cap, n_z),
        out_shape=[jax.ShapeDtypeStruct((n * cap, width), BF)] * n,
        in_specs=[pl.BlockSpec(memory_space=pltpu.SMEM), vmem, vmem],
        out_specs=[vmem] * n,
        compiler_params=pltpu.CompilerParams(vmem_limit_bytes=24 * 1024 * 1024),
        cost_estimate=pl.CostEstimate(flops=own.size, bytes_accessed=6 * own.size, transcendentals=0),
    )(place, own, came)


def total(parts):
    out = parts[0].astype(F32)
    for part in parts[1:]:
        out = out + part.astype(F32)
    return out


def reduce_rows(own, other):
    n = lax.axis_size("y")
    came = shift(other, "core", 1)
    parts = add_and_pack(own, came)
    cap = own.shape[0] // n
    once = total([parts[0]] + [crossed(parts[s], s, 0) for s in range(1, n)]).astype(BF)
    blocks = [once[s * cap : (s + 1) * cap] for s in range(n)]
    return total([blocks[0]] + [crossed(blocks[s], s, 1) for s in range(1, n)])


def to_tokens(rows, combine):
    n_z = lax.axis_size("z")
    cap = rows.shape[0]
    lanes = rows.shape[1] // n_z
    sent = rows.astype(BF).reshape(cap, n_z, lanes).transpose(1, 0, 2)
    came = lax.all_to_all(sent, "z", 0, 0, tiled=True)
    return jnp.dot(combine, came.reshape(n_z * cap, lanes), preferred_element_type=F32).astype(BF)


def shards(
    tokens,
    routed_experts,
    choice_weights,
    gate_up_weight,
    down_weight,
    adapter_first_factors,
    adapter_second_factors,
    cotangent,
):
    n_y, n_c, n_z, n_x = (lax.axis_size(a) for a in ("y", "core", "z", "x"))
    y, core, z, x = (lax.axis_index(a) for a in ("y", "core", "z", "x"))
    tok_count, width = tokens.shape
    cap = tok_count // 2
    rank = adapter_second_factors.shape[1]
    member_cols = rank // n_x

    first_here = lax.dynamic_slice_in_dim(adapter_first_factors, z * rank, rank, 2)
    first_here = jnp.concatenate([first_here[0], first_here[1]], axis=1)
    first_full = lax.all_gather(first_here, ("y", "core"), axis=0, tiled=True)

    experts = jnp.arange(n_z, dtype=jnp.int32)
    hits = routed_experts[:, :, None] == experts
    chosen = jnp.any(hits, axis=1)
    weight = jnp.sum(jnp.where(hits, choice_weights[:, :, None], 0.0), axis=1)
    earlier = jnp.arange(tok_count)[:, None] > jnp.arange(tok_count)[None, :]
    placed = jnp.dot(earlier.astype(BF), chosen.astype(BF), preferred_element_type=F32).astype(jnp.int32)
    slots = jnp.arange(cap, dtype=jnp.int32)
    here = experts == z
    chosen_here = jnp.any(chosen & here, axis=1)
    placed_here = jnp.sum(jnp.where(here, placed, 0), axis=1)
    weight_here = jnp.sum(jnp.where(here, weight, 0.0), axis=1)
    pick = (placed_here[None, :] == slots[:, None]) & chosen_here[None, :]
    row_gate = jnp.sum(jnp.where(pick, weight_here[None, :], 0.0), axis=1)
    pick = pick.astype(BF)
    combine = (placed[:, :, None] == slots) & chosen[:, :, None]
    combine = combine.astype(BF).reshape(tok_count, n_z * cap)

    x_rows = jnp.dot(pick, tokens, preferred_element_type=F32).astype(BF)
    dy_rows = (jnp.dot(pick, cotangent, preferred_element_type=F32) * row_gate[:, None]).astype(BF)

    all_x = gather_rows(x_rows)
    all_dy = gather_rows(dy_rows)
    rows = all_x.shape[0]
    mine = rows // 2

    low = jnp.dot(all_x, first_full, preferred_element_type=F32).astype(BF)
    low_halves = low.reshape(rows, 2, rank)
    pre = jnp.einsum("cd,mdf->cmf", all_x, gate_up_weight, preferred_element_type=F32)
    pre = pre + ADAPTER_SCALE * jnp.einsum(
        "cmk,mkf->cmf", low_halves, adapter_second_factors, preferred_element_type=F32
    )
    gate, up = pre[:, 0], pre[:, 1]
    sig = jax.nn.sigmoid(gate)
    hidden = (gate * sig * up).astype(BF)
    out_other = jnp.dot(hidden[mine:], down_weight, preferred_element_type=F32).astype(BF)
    out_own = jnp.dot(hidden[:mine], down_weight, preferred_element_type=F32).astype(BF)

    grad_hidden = lax.dot_general(all_dy, down_weight, (((1,), (1,)), ((), ())), preferred_element_type=F32)
    grad_gate = grad_hidden * up * sig * (1.0 + gate * (1.0 - sig))
    grad_up = grad_hidden * gate * sig
    grad_pre = jnp.stack([grad_gate, grad_up], axis=1).astype(BF)
    grad_low = ADAPTER_SCALE * jnp.einsum(
        "cmf,mkf->cmk", grad_pre, adapter_second_factors, preferred_element_type=F32
    )
    grad_low = grad_low.reshape(rows, 2 * rank)
    grad_low_half = grad_low.astype(BF)

    def back(part):
        got = jnp.einsum("cmf,mdf->cd", grad_pre[part], gate_up_weight, preferred_element_type=F32)
        got = got + lax.dot_general(
            grad_low_half[part], first_full, (((1,), (1,)), ((), ())), preferred_element_type=F32
        )
        return got.astype(BF)

    in_other = back(slice(mine, None))
    in_own = back(slice(0, mine))

    second_gradient = ADAPTER_SCALE * jnp.einsum(
        "cmk,cmf->mkf", low_halves, grad_pre, preferred_element_type=F32
    )

    mixed_rows = reduce_rows(out_own, out_other) * row_gate[:, None]
    mixed = to_tokens(mixed_rows, combine)
    token_gradient = to_tokens(reduce_rows(in_own, in_other), combine)

    def reorder(values, back_to_own):
        v = values.reshape(n_c, n_y, cap, values.shape[-1])
        start = y if back_to_own else lax.rem(n_y - y, n_y)
        if not back_to_own:
            v = jnp.where(core == 0, v, v[::-1])
        v = lax.dynamic_slice_in_dim(jnp.concatenate([v, v], axis=1), start, n_y, 1)
        if back_to_own:
            v = jnp.where(core == 0, v, v[::-1])
        return v.reshape(values.shape)

    ordered = reorder(grad_low, False).reshape(rows, 2, n_x, member_cols)
    ordered = ordered.transpose(2, 0, 1, 3).reshape(n_x, rows * 2 * member_cols // 128, 128)
    part = lax.psum_scatter(ordered, "x", scatter_dimension=0, tiled=False)
    parts = lax.all_gather(part, ("y", "core"), axis=0)
    summed = jnp.sum(parts, axis=0).reshape(rows, 2 * member_cols)
    summed = reorder(summed.astype(BF), True)
    part_width = width // (n_y * n_c)
    x_part = lax.dynamic_slice_in_dim(all_x, (y * n_c + core) * part_width, part_width, 1)
    first_gradient = lax.dot_general(
        x_part, summed.reshape(rows, 2, member_cols), (((0,), (0,)), ((), ())), preferred_element_type=F32
    ).transpose(1, 0, 2)
    return (mixed, token_gradient, first_gradient, second_gradient)


def solution(mesh):
    n_y, n_x = 4, 4
    n_dp, n_et = mesh.devices.shape
    fine = Mesh(
        mesh.devices.reshape(n_y, n_dp // n_y, n_et // n_x, n_x), ("y", "core", "z", "x")
    )
    dp, et = ("y", "core"), ("z", "x")
    both = et + dp
    return jax.shard_map(
        shards,
        mesh=fine,
        in_specs=(
            P(dp, None),
            P(dp, None),
            P(dp, None),
            P(None, None, both),
            P(both, None),
            P(None, dp, None),
            P(None, None, both),
            P(dp, None),
        ),
        out_specs=(P(dp, et), P(dp, et), P(None, dp, et), P(None, None, both)),
        check_vma=False,
    )
```

```python
import functools

import jax
import jax.numpy as jnp
from jax import lax
from jax.experimental import pallas as pl
from jax.experimental.pallas import tpu as pltpu
from jax.sharding import Mesh, PartitionSpec as P

ADAPTER_SCALE = 0.5
BF = jnp.bfloat16
F32 = jnp.float32


NT = (((1,), (1,)), ((), ()))
TN = (((0,), (0,)), ((), ()))
NN = (((1,), (0,)), ((), ()))
VMEM = pl.BlockSpec(memory_space=pltpu.VMEM)
HBM = pl.BlockSpec(memory_space=pl.ANY)
SMEM = pl.BlockSpec(memory_space=pltpu.SMEM)


def dot(a, b, dims=NN):
    return lax.dot_general(a, b, dims, preferred_element_type=F32)


def shape(dims, dtype=BF):
    return jax.ShapeDtypeStruct(dims, dtype)


def call(kernel, out_shape, inputs, in_specs, out_specs, scratch=(), name=None, limit=60, flops=0):
    return pl.pallas_call(
        kernel,
        out_shape=out_shape,
        in_specs=in_specs,
        out_specs=out_specs,
        scratch_shapes=list(scratch),
        compiler_params=pltpu.CompilerParams(vmem_limit_bytes=limit * 1024 * 1024),
        cost_estimate=pl.CostEstimate(flops=flops, bytes_accessed=0, transcendentals=0),
        name=name,
    )(*inputs)


def start(source, target, sem):
    copy = pltpu.make_async_copy(source, target, sem)
    copy.start()
    return copy


def tie(value, *earlier):
    return lax.optimization_barrier((value, *earlier))[0]


def swap(values):
    return lax.ppermute(values, "core", [(0, 1), (1, 0)])


def ahead(values, step=1):
    n_y = lax.axis_size("y")
    pairs = [(2 * y + c, 2 * ((y + step * (1 - 2 * c)) % n_y) + c) for y in range(n_y) for c in range(2)]
    return lax.ppermute(values, ("y", "core"), pairs)


def crossed(values, step, first):
    n_y, n_x = lax.axis_size("y"), lax.axis_size("x")
    pairs = []
    for y in range(n_y):
        for c in range(2):
            for x in range(n_x):
                to = ((y + step * (1 - 2 * c)) % n_y, x) if c == first else (y, (x + step) % n_x)
                pairs.append(((y * 2 + c) * n_x + x, (to[0] * 2 + c) * n_x + to[1]))
    return lax.ppermute(values, ("y", "core", "x"), pairs)


def rows_kernel(
    rank, place, tokens, cotangent, first, experts, values, out_o, far_o, gate_o, tokens_v, cotangent_v, first_v, out, sems
):
    copies = [
        start(a, b, sems.at[i])
        for i, (a, b) in enumerate(((first, first_v), (tokens, tokens_v), (cotangent, cotangent_v)))
    ]
    cap, extra = gate_o.shape[0], far_o.shape[0]
    count = 2 * cap
    hits = [experts[j : j + 1, :] == place[3] for j in range(2)]
    weight = sum(jnp.where(hit, values[j : j + 1, :], 0.0) for j, hit in enumerate(hits))
    named = jnp.where(hits[0] | hits[1], 1.0, 0.0)
    before = lax.broadcasted_iota(jnp.int32, (count, count), 0) < lax.broadcasted_iota(jnp.int32, (count, count), 1)
    placed = dot(jnp.broadcast_to(named, (8, count)).astype(BF), jnp.where(before, 1.0, 0.0).astype(BF))[:1, :]
    slot = lax.broadcasted_iota(jnp.int32, (cap, count), 0)
    match = (jnp.broadcast_to(placed, (cap, count)).astype(jnp.int32) == slot) & (
        jnp.broadcast_to(named, (cap, count)) > 0.5
    )
    gate = jnp.sum(jnp.where(match, jnp.broadcast_to(weight, (cap, count)), 0.0), axis=1, keepdims=True)
    gate_o[...] = gate
    pick = jnp.where(match, 1.0, 0.0).astype(BF)
    n, cols = first.shape[1], first.shape[2]
    row = lax.broadcasted_iota(jnp.int32, (2 * rank, cols), 0)
    col = lax.broadcasted_iota(jnp.int32, (2 * rank, cols), 1)
    copies[0].wait()
    held = None
    for m in range(2):
        take = (col == place[3] * rank + row - m * rank) & (row >= m * rank) & (row < (m + 1) * rank)
        term = dot(jnp.where(take, 1.0, 0.0).astype(BF), first_v[m], NT)
        held = term if held is None else held + term
    held = held.astype(BF)
    for j in range(2 * rank // extra):
        piece = held[j * extra : (j + 1) * extra, :]
        out[cap : cap + extra, j * n : (j + 1) * n] = piece
    far_copy = start(out.at[pl.ds(cap, extra), :], far_o, sems.at[3])
    copies[1].wait()
    out[:cap, :] = dot(pick, tokens_v[...]).astype(BF)
    copies[2].wait()
    out[cap + extra :, :] = (dot(pick, cotangent_v[...]) * gate).astype(BF)
    start(out, out_o, sems.at[4]).wait()
    far_copy.wait()


def expert_rows(tokens, cotangent, first, experts, values, rank, place):
    count, width = tokens.shape
    cap = count // 2
    extra = first.shape[1] * 2 * rank // width
    return call(
        functools.partial(rows_kernel, rank),
        [shape((2 * cap + extra, width)), shape((extra, width)), shape((cap, 1), F32)],
        [place, tokens, cotangent, first, experts, values],
        [SMEM, HBM, HBM, HBM, VMEM, VMEM],
        [HBM, HBM, VMEM],
        scratch=[
            pltpu.VMEM(tokens.shape, BF),
            pltpu.VMEM(cotangent.shape, BF),
            pltpu.VMEM(first.shape, BF),
            pltpu.VMEM((2 * cap + extra, width), BF),
            pltpu.SemaphoreType.DMA((5,)),
        ],
        name="expert_rows",
    )


N_Y = 4
CHUNK = 1024


def block_of(place, k, other):
    y, core = place[0], place[1]
    way = 1 - 2 * core
    return lax.rem(y + way * k + 2 * N_Y, N_Y) * 2 + (1 - core if other else core)


def wait(copies):
    for c in copies:
        c.wait()


def chunk_copies(i, outs, mine, other, sems):
    cols = pl.ds(pl.multiple_of(i * CHUNK, CHUNK), CHUNK)
    half = mine.shape[0]
    return [
        pltpu.make_async_copy(outs.at[pl.ds(half, half), cols], other.at[:, cols], sems.at[2 * i]),
        pltpu.make_async_copy(outs.at[pl.ds(0, half), cols], mine.at[:, cols], sems.at[2 * i + 1]),
    ]


def write_chunks(product, outs, mine, other, sems):
    def step(i, carry):
        product(pl.ds(pl.multiple_of(i * CHUNK, CHUNK), CHUNK))
        for c in chunk_copies(i, outs, mine, other, sems):
            c.start()
        return carry

    lax.fori_loop(0, outs.shape[1] // CHUNK, step, 0)


def finish_chunks(outs, mine, other, sems):
    def step(i, carry):
        wait(chunk_copies(i, outs, mine, other, sems))
        return carry

    lax.fori_loop(0, outs.shape[1] // CHUNK, step, 0)


def preactivations(xs, weights, second):
    h, rank = second.shape[2], second.shape[1]
    pre = dot(xs[...], weights[...], NT)
    low = pre[:, 2 * h :].astype(BF)
    gate = pre[:, :h] + ADAPTER_SCALE * dot(low[:, :rank], second[0])
    up = pre[:, h : 2 * h] + ADAPTER_SCALE * dot(low[:, rank:], second[1])
    return gate, up, low, (gate / (1.0 + jnp.exp(-gate)) * up).astype(BF)


def forward_kernel(cap, steps, place, *refs):
    n = 2 * len(steps)
    blocks, fars, (gate_up, down, second), refs = refs[:n], refs[n : n + 2], refs[n + 2 : n + 5], refs[n + 5 :]
    (gate_o, up_o, low_o, mine, other, first_out), refs = refs[:6], refs[6:]
    xs, weights, down_v, hidden, gate_v, up_v, low_v, packed, outs, in_sems, out_sems = refs
    h, rank, width = down.shape[0], second.shape[1], down.shape[1]
    lanes, extra = 2 * rank, fars[0].shape[0]
    first = weights.at[pl.ds(2 * h, lanes), :]
    count = iter(range(64))

    def fetch(source, target):
        return start(source, target, in_sems.at[next(count)])

    sources = [b.at[pl.ds(cap, extra), :] for b in blocks] + list(fars)
    got_first = [fetch(a, packed.at[pl.ds(i * extra, extra), :]) for i, a in enumerate(sources)]
    got_x = [fetch(b.at[pl.ds(0, cap), :], xs.at[pl.ds(i * cap, cap), :]) for i, b in enumerate(blocks)]
    got_gate_up = fetch(gate_up, weights.at[pl.ds(0, 2 * h), :])
    got_down = fetch(down, down_v)

    wait(got_first)
    step = extra * width // lanes
    held = [(k, o) for o in (False, True) for k in steps] + [(2, False), (2, True)]
    for i, (k, o) in enumerate(held):
        at = pl.ds(pl.multiple_of(block_of(place, k, o) * step, step), step)
        for j in range(lanes // extra):
            piece = packed[i * extra : (i + 1) * extra, j * step : (j + 1) * step]
            weights[2 * h + j * extra : 2 * h + (j + 1) * extra, at] = piece
    save = [start(first, first_out, out_sems.at[8])]
    wait(got_x)
    got_gate_up.wait()
    gate, up, low, act = preactivations(xs, weights, second)
    gate_v[...] = gate
    up_v[...] = up
    low_v[...] = low
    hidden[...] = act
    for i, (a, b) in enumerate(((gate_v, gate_o), (up_v, up_o), (low_v, low_o))):
        save.append(start(a, b, out_sems.at[9 + i]))
    got_down.wait()

    def product(cols):
        outs[:, cols] = dot(hidden[...], down_v[:, cols]).astype(BF)

    write_chunks(product, outs, mine, other, out_sems)
    finish_chunks(outs, mine, other, out_sems)
    wait(save)


def forward(cap, steps, place, blocks, fars, gate_up, down, second):
    n, width, h, both = len(blocks), down.shape[1], down.shape[0], 2 * second.shape[1]
    rows = n * cap
    return call(
        functools.partial(forward_kernel, cap, steps),
        [
            shape((rows, h), F32),
            shape((rows, h), F32),
            shape((rows, both)),
            shape((rows // 2, width)),
            shape((rows // 2, width)),
            shape((both, width)),
        ],
        [place, *blocks, *fars, gate_up, down, second],
        [SMEM] + [HBM] * (n + 4) + [VMEM],
        [HBM] * 6,
        scratch=[
            pltpu.VMEM((rows, width), BF),
            pltpu.VMEM((2 * h + both, width), BF),
            pltpu.VMEM(down.shape, BF),
            pltpu.VMEM((rows, h), BF),
            pltpu.VMEM((rows, h), F32),
            pltpu.VMEM((rows, h), F32),
            pltpu.VMEM((rows, both), BF),
            pltpu.VMEM(((n + 2) * fars[0].shape[0], width), BF),
            pltpu.VMEM((rows, width), BF),
            pltpu.SemaphoreType.DMA((2 * n + 4,)),
            pltpu.SemaphoreType.DMA((12,)),
        ],
        flops=10**10,
        name="forward_rows",
    )


def rest_kernel(cap, place, *refs):
    near, far_x, far_d, refs = refs[:6], refs[6:8], refs[8:10], refs[10:]
    (gate_n, up_n, low_n, gate_up, down, first, second), refs = refs[:7], refs[7:]
    (low_a, low_b, part, second_o, mine, other), refs = refs[:6], refs[6:]
    xs, ds, gate_v, up_v, low_v, weights, down_v, hidden, grads, outs, in_sems, out_sems = refs
    h, rank, width = down.shape[0], second.shape[1], down.shape[1]
    n = 2 * N_Y
    half = N_Y * cap
    count = iter(range(64))

    def fetch(source, target):
        return start(source, target, in_sems.at[next(count)])

    def rows_of(i):
        return pl.ds(i * cap, cap)

    place_of = {}
    for o in range(2):
        for j, k in enumerate((0, 1, 3)):
            place_of[o * N_Y + k] = (False, 3 * o + j)
        place_of[o * N_Y + 2] = (True, o)
    last = near[0].shape[0] - cap
    got_x = [fetch(far_x[o].at[pl.ds(0, cap), :], xs.at[rows_of(o), :]) for o in range(2)]
    got_weights = [fetch(gate_up, weights.at[pl.ds(0, 2 * h), :]), fetch(first, weights.at[pl.ds(2 * h, 2 * rank), :])]
    got_down = fetch(down, down_v)
    got_d, got_pre, saved = [], [], []
    for i in range(n):
        is_far, j = place_of[i]
        got_d.append(fetch(far_d[j] if is_far else near[j].at[pl.ds(last, cap), :], ds.at[rows_of(i), :]))
    for i in range(n):
        is_far, j = place_of[i]
        if not is_far:
            for source, target in ((gate_n, gate_v), (up_n, up_v), (low_n, low_v)):
                got_pre.append(fetch(source.at[rows_of(j), :], target.at[rows_of(i), :]))
    step = part.shape[1]
    cols = pl.ds(pl.multiple_of((place[0] * 2 + place[1]) * step, step), step)
    for i in range(n):
        is_far, j = place_of[i]
        at = pl.multiple_of(block_of(place, i % N_Y, i >= N_Y) * cap, cap)
        source = (far_x if is_far else near)[j].at[pl.ds(0, cap), cols]
        saved.append(start(source, part.at[pl.ds(at, cap), :], out_sems.at[8 + i]))

    wait(got_x)
    wait(got_weights)
    gate, up, low, act = preactivations(xs, weights, second)
    hidden[...] = act
    for o in range(2):
        to = (o * N_Y + 2) * cap
        for value, target in ((gate, gate_v), (up, up_v), (low, low_v)):
            target[to : to + cap, :] = value[o * cap : (o + 1) * cap, :]

    got_down.wait()
    wait(got_d)
    grad = dot(ds[...], down_v[...], NT)
    wait(got_pre)
    gate, up = gate_v[...], up_v[...]
    sig = 1.0 / (1.0 + jnp.exp(-gate))
    grad_gate = (grad * up * sig * (1.0 + gate * (1.0 - sig))).astype(BF)
    grad_up = (grad * gate * sig).astype(BF)
    both = [ADAPTER_SCALE * dot(grad_gate, second[0], NT), ADAPTER_SCALE * dot(grad_up, second[1], NT)]
    grad_low = jnp.concatenate(both, axis=1).astype(BF)
    grads[...] = jnp.concatenate([grad_gate, grad_up, grad_low], axis=1)

    def product(cols):
        got = dot(hidden[...], down_v[:, cols]).astype(BF)
        back = dot(grads[...], weights[:, cols]).astype(BF)
        for o in range(2):
            base = o * (half + cap)
            outs[base : base + cap, cols] = got[o * cap : (o + 1) * cap, :]
            outs[base + cap : base + cap + half, cols] = back[o * half : (o + 1) * half, :]

    write_chunks(product, outs, mine, other, out_sems)
    second_o[0] = ADAPTER_SCALE * dot(low_v[:, :rank], grad_gate, TN)
    second_o[1] = ADAPTER_SCALE * dot(low_v[:, rank:], grad_up, TN)

    lanes = 2 * rank
    row = lax.broadcasted_iota(jnp.int32, (lanes, lanes), 0)
    col = lax.broadcasted_iota(jnp.int32, (lanes, lanes), 1)
    members = rank // 4
    away, factor, member = row // (2 * members), (row // members) % 2, row % members
    wanted = factor * rank + (place[2] ^ away) * members + member
    order = jnp.where(wanted == col, 1.0, 0.0).astype(BF)
    straight = place[1] == 0
    for k in range(N_Y):
        ours = grad_low[k * cap : (k + 1) * cap, :].astype(F32)
        theirs = grad_low[(N_Y + k) * cap : (N_Y + k + 1) * cap, :].astype(F32)
        rows = jnp.concatenate([jnp.where(straight, ours, theirs), jnp.where(straight, theirs, ours)], axis=0)
        turned = dot(order, rows.astype(BF), NT).astype(BF)
        at = pl.multiple_of(lax.div(block_of(place, k, False), 2) * 2 * cap, 2 * cap)
        low_a[:, pl.ds(at, 2 * cap)] = turned[: lanes // 2, :]
        low_b[:, pl.ds(at, 2 * cap)] = turned[lanes // 2 :, :]
    finish_chunks(outs, mine, other, out_sems)
    wait(saved)


def rest(cap, place, near, far_x, far_d, pre_near, gate_up, down, first, second):
    width, h, both = down.shape[1], down.shape[0], 2 * second.shape[1]
    rows = 2 * N_Y * cap
    return call(
        functools.partial(rest_kernel, cap),
        [
            shape((both // 2, rows)),
            shape((both // 2, rows)),
            shape((rows, width // (2 * N_Y))),
            shape(second.shape, F32),
            shape((rows // 2 + cap, width)),
            shape((rows // 2 + cap, width)),
        ],
        [place, *near, *far_x, *far_d, *pre_near, gate_up, down, first, second],
        [SMEM] + [HBM] * 16 + [VMEM],
        [VMEM, VMEM, HBM, VMEM, HBM, HBM],
        scratch=[
            pltpu.VMEM((2 * cap, width), BF),
            pltpu.VMEM((rows, width), BF),
            pltpu.VMEM((rows, h), F32),
            pltpu.VMEM((rows, h), F32),
            pltpu.VMEM((rows, both), BF),
            pltpu.VMEM((2 * h + both, width), BF),
            pltpu.VMEM(down.shape, BF),
            pltpu.VMEM((2 * cap, h), BF),
            pltpu.VMEM((rows, 2 * h + both), BF),
            pltpu.VMEM((rows + 2 * cap, width), BF),
            pltpu.SemaphoreType.DMA((8 * N_Y + 3,)),
            pltpu.SemaphoreType.DMA((8 + 2 * N_Y,)),
        ],
        flops=10**10,
        name="rest_rows",
    )


def pack_kernel(cap, n_z, place, *refs):
    sources, outs, (own, came, packed, sems, out_sems) = refs[:4], refs[4 : 4 + 2 * N_Y], refs[4 + 2 * N_Y :]
    n = N_Y
    core, x = place[1], place[2]
    lanes = own.shape[2] // (n_z * n)
    copies = []
    for which in range(2):
        for k in range(n):
            for i, target in enumerate((own, came)):
                near, last = sources[2 * i], sources[2 * i + 1]
                if which:
                    source = last.at[pl.ds((1 + k) * cap, cap), :]
                elif k == 2:
                    source = last.at[pl.ds(0, cap), :]
                else:
                    source = near.at[pl.ds(min(k, 2) * cap, cap), :]
                to = target.at[which, pl.ds(k * cap, cap), :]
                copies.append(start(source, to, sems.at[len(copies)]))

    def block(which, i, q, z):
        cols = pl.ds(pl.multiple_of(z * n * lanes + lax.rem(x + q, n) * lanes, lanes), lanes)
        here = own[which, i * cap : (i + 1) * cap, cols].astype(F32)
        j = (n - i) % n
        return (here + came[which, j * cap : (j + 1) * cap, cols].astype(F32)).astype(BF)

    def store(which, straight):
        for to in range(n):
            for slot in range(n):
                i, q = (to, slot) if straight else (slot, to)
                for z in range(n_z):
                    rows, cols = slice(slot * cap, (slot + 1) * cap), slice(z * lanes, (z + 1) * lanes)
                    packed[which * n + to, rows, cols] = block(which, i, q, z)
            start(packed.at[which * n + to], outs[which * n + to], out_sems.at[which * n + to])

    for which in range(2):
        wait(copies[which * 2 * n : (which + 1) * 2 * n])

        @pl.when(core == 0)
        def _():
            store(which, True)

        @pl.when(core == 1)
        def _():
            store(which, False)

    for to in range(2 * n):
        pltpu.make_async_copy(packed.at[to], outs[to], out_sems.at[to]).wait()


def add_and_pack(cap, sources, place):
    n, n_z = N_Y, lax.axis_size("z")
    width = sources[0].shape[1]
    parts = call(
        functools.partial(pack_kernel, cap, n_z),
        [shape((n * cap, width // n))] * (2 * n),
        [place, *sources],
        [SMEM] + [HBM] * len(sources),
        [HBM] * (2 * n),
        scratch=[pltpu.VMEM((2, n * cap, width), BF)] * 2
        + [
            pltpu.VMEM((2 * n, n * cap, width // n), BF),
            pltpu.SemaphoreType.DMA((4 * n,)),
            pltpu.SemaphoreType.DMA((2 * n,)),
        ],
        limit=20,
        name="add_and_pack",
    )
    return parts[:n], parts[n:]


def total(parts):
    out = parts[0].astype(F32)
    for part in parts[1:]:
        out = out + part.astype(F32)
    return out


def first_moves(parts):
    return [parts[0]] + [crossed(parts[s], s, 0) for s in range(1, len(parts))]


def second_moves(once, n):
    cap = once.shape[0] // n
    blocks = [once[s * cap : (s + 1) * cap] for s in range(n)]
    return [blocks[0]] + [crossed(blocks[s], s, 1) for s in range(1, n)]


def to_tokens(rows, combine):
    n_z = lax.axis_size("z")
    cap = rows[0].shape[0]
    lanes = rows[0].shape[1] // n_z
    sent = [r.astype(BF).reshape(cap, n_z, lanes).transpose(1, 0, 2) for r in rows]
    came = lax.all_to_all(jnp.concatenate(sent, axis=2), "z", 0, 0, tiled=True)
    came = came.reshape(n_z * cap, len(rows) * lanes)
    sums = dot(combine, came).astype(BF)
    return [sums[:, i * lanes : (i + 1) * lanes] for i in range(len(rows))]


def shards(
    tokens,
    routed_experts,
    choice_weights,
    gate_up_weight,
    down_weight,
    adapter_first_factors,
    adapter_second_factors,
    cotangent,
):
    n_y, n_c, n_z, n_x = (lax.axis_size(a) for a in ("y", "core", "z", "x"))
    y, core, z, x = (lax.axis_index(a) for a in ("y", "core", "z", "x"))
    tok_count, width = tokens.shape
    cap = tok_count // 2
    rank = adapter_second_factors.shape[1]
    member_cols = rank // n_x
    hidden_count = down_weight.shape[0]
    part_width = width // (n_y * n_c)
    gate_up = gate_up_weight.swapaxes(1, 2).reshape(2 * hidden_count, width)

    place = jnp.stack([y, core, x, z]).astype(jnp.int32)
    own, far_first, row_gate = expert_rows(
        tokens, cotangent, adapter_first_factors, routed_experts.T, choice_weights.T, rank, place
    )
    chosen = jnp.any(routed_experts[:, :, None] == jnp.arange(n_z, dtype=jnp.int32), axis=1)
    earlier = jnp.arange(tok_count)[:, None] > jnp.arange(tok_count)[None, :]
    placed = dot(earlier.astype(BF), chosen.astype(BF)).astype(jnp.int32)
    combine = (placed[:, :, None] == jnp.arange(cap, dtype=jnp.int32)) & chosen[:, :, None]
    combine = combine.astype(BF).reshape(tok_count, n_z * cap)

    behind = ahead(own)
    front = ahead(own, -1)
    own_s = swap(own)
    far_first = ahead(far_first, 2)
    front_s = swap(behind)
    behind_s = swap(front)
    far_first_s = swap(far_first)
    relayed = tie(behind, front_s, behind_s, far_first_s)
    far_x = ahead(relayed[: own.shape[0] - cap])
    far_d = ahead(relayed[own.shape[0] - cap :])

    weights = (gate_up, down_weight)
    near = [own, front, behind, own_s, front_s, behind_s]
    *pre_near, mine_near, other_near, first = forward(
        cap, (0, 1, 3), place, near, [far_first, far_first_s], *weights, adapter_second_factors
    )
    came_near = swap(other_near)
    far_x, far_d, _ = lax.optimization_barrier((far_x, far_d, mine_near))
    far_x_s = swap(far_x)
    far_d_s = swap(far_d)
    low_a, low_b, x_part, second_gradient, mine_rest, other_rest = rest(
        cap, place, near, [far_x, far_x_s], [far_d, far_d_s], pre_near, *weights, first, adapter_second_factors
    )
    came_rest = swap(other_rest)

    def crossing(axis, bit):
        return [(i, i ^ bit) for i in range(lax.axis_size(axis))]

    cols = low_a.shape[0] // 2
    pair = low_a.astype(F32) + lax.ppermute(low_b, "x", crossing("x", 2)).astype(F32)
    low_sum = pair[:cols] + lax.ppermute(pair[cols:].astype(BF), "x", crossing("x", 1)).astype(F32)
    out_parts, in_parts = add_and_pack(cap, [mine_near, mine_rest, came_near, came_rest], place)
    out_got = first_moves(out_parts)
    in_got = first_moves(in_parts)
    out_once = total(out_got).astype(BF)
    mixed_rows = total(second_moves(out_once, n_y)) * row_gate
    low_sum = low_sum + swap(tie(low_sum, *in_got))
    in_once = tie(total(in_got).astype(BF), low_sum)
    in_moved = second_moves(in_once, n_y)
    low_sum = tie(low_sum, in_moved[1])
    low_sum = low_sum + lax.ppermute(low_sum, "y", crossing("y", 2))
    in_rows = tie(total(in_moved), low_sum)
    mixed, token_gradient = to_tokens([mixed_rows, in_rows], combine)
    summed = (low_sum + lax.ppermute(low_sum, "y", crossing("y", 1))).astype(BF)
    first_gradient = dot(summed, x_part).reshape(2, member_cols, part_width).transpose(0, 2, 1)
    return (mixed, token_gradient, first_gradient, second_gradient)


def solution(mesh):
    n_y, n_x = 4, 4
    n_dp, n_et = mesh.devices.shape
    fine = Mesh(
        mesh.devices.reshape(n_y, n_dp // n_y, n_et // n_x, n_x), ("y", "core", "z", "x")
    )
    dp, et = ("y", "core"), ("z", "x")
    both = et + dp
    return jax.shard_map(
        shards,
        mesh=fine,
        in_specs=(
            P(dp, None),
            P(dp, None),
            P(dp, None),
            P(None, None, both),
            P(both, None),
            P(None, dp, None),
            P(None, None, both),
            P(dp, None),
        ),
        out_specs=(P(dp, et), P(dp, et), P(None, dp, et), P(None, None, both)),
        check_vma=False,
    )
```

```python
import functools

import jax
import jax.numpy as jnp
from jax import lax
from jax.experimental import pallas as pl
from jax.experimental.pallas import tpu as pltpu
from jax.sharding import Mesh, PartitionSpec as P

ADAPTER_SCALE = 0.5
BF = jnp.bfloat16
F32 = jnp.float32


NT = (((1,), (1,)), ((), ()))
TN = (((0,), (0,)), ((), ()))
NN = (((1,), (0,)), ((), ()))
VMEM = pl.BlockSpec(memory_space=pltpu.VMEM)
HBM = pl.BlockSpec(memory_space=pl.ANY)
SMEM = pl.BlockSpec(memory_space=pltpu.SMEM)


def dot(a, b, dims=NN):
    return lax.dot_general(a, b, dims, preferred_element_type=F32)


def shape(dims, dtype=BF):
    return jax.ShapeDtypeStruct(dims, dtype)


def call(kernel, out_shape, inputs, in_specs, out_specs, scratch=(), name=None, limit=60, flops=0):
    return pl.pallas_call(
        kernel,
        out_shape=out_shape,
        in_specs=in_specs,
        out_specs=out_specs,
        scratch_shapes=list(scratch),
        compiler_params=pltpu.CompilerParams(vmem_limit_bytes=limit * 1024 * 1024),
        cost_estimate=pl.CostEstimate(flops=flops, bytes_accessed=0, transcendentals=0),
        name=name,
    )(*inputs)


def start(source, target, sem):
    copy = pltpu.make_async_copy(source, target, sem)
    copy.start()
    return copy


def tie(value, *earlier):
    return lax.optimization_barrier((value, *earlier))[0]


def swap(values):
    return lax.ppermute(values, "core", [(0, 1), (1, 0)])


def ahead(values, step=1):
    n_y = lax.axis_size("y")
    pairs = [(2 * y + c, 2 * ((y + step * (1 - 2 * c)) % n_y) + c) for y in range(n_y) for c in range(2)]
    return lax.ppermute(values, ("y", "core"), pairs)


def crossed(values, step, first):
    n_y, n_x = lax.axis_size("y"), lax.axis_size("x")
    pairs = []
    for y in range(n_y):
        for c in range(2):
            for x in range(n_x):
                to = ((y + step * (1 - 2 * c)) % n_y, x) if c == first else (y, (x + step) % n_x)
                pairs.append(((y * 2 + c) * n_x + x, (to[0] * 2 + c) * n_x + to[1]))
    return lax.ppermute(values, ("y", "core", "x"), pairs)


def rows_kernel(
    rank, place, tokens, cotangent, first, experts, values, out_o, far_o, gate_o, tokens_v, cotangent_v, first_v, out, sems
):
    copies = [
        start(a, b, sems.at[i])
        for i, (a, b) in enumerate(((first, first_v), (tokens, tokens_v), (cotangent, cotangent_v)))
    ]
    cap, extra = gate_o.shape[0], far_o.shape[0]
    count = 2 * cap
    hits = [experts[j : j + 1, :] == place[3] for j in range(2)]
    weight = sum(jnp.where(hit, values[j : j + 1, :], 0.0) for j, hit in enumerate(hits))
    named = jnp.where(hits[0] | hits[1], 1.0, 0.0)
    before = lax.broadcasted_iota(jnp.int32, (count, count), 0) < lax.broadcasted_iota(jnp.int32, (count, count), 1)
    placed = dot(jnp.broadcast_to(named, (8, count)).astype(BF), jnp.where(before, 1.0, 0.0).astype(BF))[:1, :]
    slot = lax.broadcasted_iota(jnp.int32, (cap, count), 0)
    match = (jnp.broadcast_to(placed, (cap, count)).astype(jnp.int32) == slot) & (
        jnp.broadcast_to(named, (cap, count)) > 0.5
    )
    gate = jnp.sum(jnp.where(match, jnp.broadcast_to(weight, (cap, count)), 0.0), axis=1, keepdims=True)
    gate_o[...] = gate
    pick = jnp.where(match, 1.0, 0.0).astype(BF)
    n, cols = first.shape[1], first.shape[2]
    row = lax.broadcasted_iota(jnp.int32, (2 * rank, cols), 0)
    col = lax.broadcasted_iota(jnp.int32, (2 * rank, cols), 1)
    copies[0].wait()
    held = None
    for m in range(2):
        take = (col == place[3] * rank + row - m * rank) & (row >= m * rank) & (row < (m + 1) * rank)
        term = dot(jnp.where(take, 1.0, 0.0).astype(BF), first_v[m], NT)
        held = term if held is None else held + term
    held = held.astype(BF)
    for j in range(2 * rank // extra):
        piece = held[j * extra : (j + 1) * extra, :]
        out[:extra, j * n : (j + 1) * n] = piece
    far_copy = start(out.at[pl.ds(0, extra), :], far_o, sems.at[3])
    copies[1].wait()
    out[extra : extra + cap, :] = dot(pick, tokens_v[...]).astype(BF)
    copies[2].wait()
    out[cap + extra :, :] = (dot(pick, cotangent_v[...]) * gate).astype(BF)
    start(out, out_o, sems.at[4]).wait()
    far_copy.wait()


def expert_rows(tokens, cotangent, first, experts, values, rank, place):
    count, width = tokens.shape
    cap = count // 2
    extra = first.shape[1] * 2 * rank // width
    return call(
        functools.partial(rows_kernel, rank),
        [shape((2 * cap + extra, width)), shape((extra, width)), shape((cap, 1), F32)],
        [place, tokens, cotangent, first, experts, values],
        [SMEM, HBM, HBM, HBM, VMEM, VMEM],
        [HBM, HBM, VMEM],
        scratch=[
            pltpu.VMEM(tokens.shape, BF),
            pltpu.VMEM(cotangent.shape, BF),
            pltpu.VMEM(first.shape, BF),
            pltpu.VMEM((2 * cap + extra, width), BF),
            pltpu.SemaphoreType.DMA((5,)),
        ],
        name="expert_rows",
    )


N_Y = 4
CHUNK = 2048


def block_of(place, k, other):
    y, core = place[0], place[1]
    way = 1 - 2 * core
    return lax.rem(y + way * k + 2 * N_Y, N_Y) * 2 + (1 - core if other else core)


def wait(copies):
    for c in copies:
        c.wait()


def chunk_copies(i, outs, mine, other, sems):
    cols = pl.ds(pl.multiple_of(i * CHUNK, CHUNK), CHUNK)
    half = mine.shape[0]
    return [
        pltpu.make_async_copy(outs.at[pl.ds(half, half), cols], other.at[:, cols], sems.at[2 * i]),
        pltpu.make_async_copy(outs.at[pl.ds(0, half), cols], mine.at[:, cols], sems.at[2 * i + 1]),
    ]


def write_chunks(product, outs, mine, other, sems):
    def step(i, carry):
        product(pl.ds(pl.multiple_of(i * CHUNK, CHUNK), CHUNK))
        for c in chunk_copies(i, outs, mine, other, sems):
            c.start()
        return carry

    lax.fori_loop(0, outs.shape[1] // CHUNK, step, 0)


def finish_chunks(outs, mine, other, sems):
    def step(i, carry):
        wait(chunk_copies(i, outs, mine, other, sems))
        return carry

    lax.fori_loop(0, outs.shape[1] // CHUNK, step, 0)


def preactivations(xs, weights, second):
    h, rank = second.shape[2], second.shape[1]
    pre = dot(xs[...], weights[...], NT)
    low = pre[:, 2 * h :].astype(BF)
    gate = pre[:, :h] + ADAPTER_SCALE * dot(low[:, :rank], second[0])
    up = pre[:, h : 2 * h] + ADAPTER_SCALE * dot(low[:, rank:], second[1])
    return gate, up, low, (gate / (1.0 + jnp.exp(-gate)) * up).astype(BF)


def forward_kernel(cap, steps, place, *refs):
    n = 2 * len(steps)
    blocks, fars, (gate_up, down, second), refs = refs[:n], refs[n : n + 2], refs[n + 2 : n + 5], refs[n + 5 :]
    (gate_o, up_o, low_o, mine, other, first_out), refs = refs[:6], refs[6:]
    xs, weights, down_v, hidden, gate_v, up_v, low_v, packed, outs, in_sems, out_sems = refs
    h, rank, width = down.shape[0], second.shape[1], down.shape[1]
    lanes, extra = 2 * rank, fars[0].shape[0]
    first = weights.at[pl.ds(2 * h, lanes), :]
    count = iter(range(64))

    def fetch(source, target):
        return start(source, target, in_sems.at[next(count)])

    sources = [b.at[pl.ds(0, extra), :] for b in blocks] + list(fars)
    got_first = [fetch(a, packed.at[pl.ds(i * extra, extra), :]) for i, a in enumerate(sources)]
    got_x = [fetch(b.at[pl.ds(extra, cap), :], xs.at[pl.ds(i * cap, cap), :]) for i, b in enumerate(blocks)]
    got_gate_up = fetch(gate_up, weights.at[pl.ds(0, 2 * h), :])
    got_down = fetch(down, down_v)

    wait(got_first)
    step = extra * width // lanes
    held = [(k, o) for o in (False, True) for k in steps] + [(2, False), (2, True)]
    for i, (k, o) in enumerate(held):
        at = pl.ds(pl.multiple_of(block_of(place, k, o) * step, step), step)
        for j in range(lanes // extra):
            piece = packed[i * extra : (i + 1) * extra, j * step : (j + 1) * step]
            weights[2 * h + j * extra : 2 * h + (j + 1) * extra, at] = piece
    save = [start(first, first_out, out_sems.at[8])]
    wait(got_x)
    got_gate_up.wait()
    gate, up, low, act = preactivations(xs, weights, second)
    gate_v[...] = gate
    up_v[...] = up
    low_v[...] = low
    hidden[...] = act
    for i, (a, b) in enumerate(((gate_v, gate_o), (up_v, up_o), (low_v, low_o))):
        save.append(start(a, b, out_sems.at[9 + i]))
    got_down.wait()

    def product(cols):
        outs[:, cols] = dot(hidden[...], down_v[:, cols]).astype(BF)

    write_chunks(product, outs, mine, other, out_sems)
    finish_chunks(outs, mine, other, out_sems)
    wait(save)


def forward(cap, steps, place, blocks, fars, gate_up, down, second):
    n, width, h, both = len(blocks), down.shape[1], down.shape[0], 2 * second.shape[1]
    rows = n * cap
    return call(
        functools.partial(forward_kernel, cap, steps),
        [
            shape((rows, h), F32),
            shape((rows, h), F32),
            shape((rows, both)),
            shape((rows // 2, width)),
            shape((rows // 2, width)),
            shape((both, width)),
        ],
        [place, *blocks, *fars, gate_up, down, second],
        [SMEM] + [HBM] * (n + 4) + [VMEM],
        [HBM] * 6,
        scratch=[
            pltpu.VMEM((rows, width), BF),
            pltpu.VMEM((2 * h + both, width), BF),
            pltpu.VMEM(down.shape, BF),
            pltpu.VMEM((rows, h), BF),
            pltpu.VMEM((rows, h), F32),
            pltpu.VMEM((rows, h), F32),
            pltpu.VMEM((rows, both), BF),
            pltpu.VMEM(((n + 2) * fars[0].shape[0], width), BF),
            pltpu.VMEM((rows, width), BF),
            pltpu.SemaphoreType.DMA((2 * n + 4,)),
            pltpu.SemaphoreType.DMA((12,)),
        ],
        flops=10**10,
        name="forward_rows",
    )


def rest_kernel(cap, place, *refs):
    near, far, refs = refs[:6], refs[6:8], refs[8:]
    (gate_n, up_n, low_n, gate_up, down, first, second), refs = refs[:7], refs[7:]
    (low_t, part, second_o, mine, other), refs = refs[:5], refs[5:]
    xs, ds, gate_v, up_v, low_v, weights, down_v, hidden, grads, outs, in_sems, out_sems = refs
    h, rank, width = down.shape[0], second.shape[1], down.shape[1]
    n = 2 * N_Y
    half = N_Y * cap
    count = iter(range(64))

    def fetch(source, target):
        return start(source, target, in_sems.at[next(count)])

    def rows_of(i):
        return pl.ds(i * cap, cap)

    place_of = {}
    for o in range(2):
        for j, k in enumerate((0, 1, 3)):
            place_of[o * N_Y + k] = (False, 3 * o + j)
        place_of[o * N_Y + 2] = (True, o)
    extra = near[0].shape[0] - 2 * cap
    got_x = [fetch(far[o].at[pl.ds(0, cap), :], xs.at[rows_of(o), :]) for o in range(2)]
    got_weights = [fetch(gate_up, weights.at[pl.ds(0, 2 * h), :]), fetch(first, weights.at[pl.ds(2 * h, 2 * rank), :])]
    got_down = fetch(down, down_v)
    got_d, got_pre, saved = [], [], []
    for i in range(n):
        is_far, j = place_of[i]
        source = far[j].at[pl.ds(cap, cap), :] if is_far else near[j].at[pl.ds(extra + cap, cap), :]
        got_d.append(fetch(source, ds.at[rows_of(i), :]))
    for i in range(n):
        is_far, j = place_of[i]
        if not is_far:
            for source, target in ((gate_n, gate_v), (up_n, up_v), (low_n, low_v)):
                got_pre.append(fetch(source.at[rows_of(j), :], target.at[rows_of(i), :]))
    step = part.shape[1]
    cols = pl.ds(pl.multiple_of((place[0] * 2 + place[1]) * step, step), step)
    for i in range(n):
        is_far, j = place_of[i]
        at = pl.multiple_of(block_of(place, i % N_Y, i >= N_Y) * cap, cap)
        source = far[j].at[pl.ds(0, cap), cols] if is_far else near[j].at[pl.ds(extra, cap), cols]
        saved.append(start(source, part.at[pl.ds(at, cap), :], out_sems.at[8 + i]))

    wait(got_x)
    wait(got_weights)
    gate, up, low, act = preactivations(xs, weights, second)
    hidden[...] = act
    for o in range(2):
        to = (o * N_Y + 2) * cap
        for value, target in ((gate, gate_v), (up, up_v), (low, low_v)):
            target[to : to + cap, :] = value[o * cap : (o + 1) * cap, :]

    got_down.wait()
    wait(got_d)
    grad = dot(ds[...], down_v[...], NT)
    wait(got_pre)
    gate, up = gate_v[...], up_v[...]
    sig = 1.0 / (1.0 + jnp.exp(-gate))
    grad_gate = (grad * up * sig * (1.0 + gate * (1.0 - sig))).astype(BF)
    grad_up = (grad * gate * sig).astype(BF)
    both = [ADAPTER_SCALE * dot(grad_gate, second[0], NT), ADAPTER_SCALE * dot(grad_up, second[1], NT)]
    grad_low = jnp.concatenate(both, axis=1).astype(BF)
    grads[...] = jnp.concatenate([grad_gate, grad_up, grad_low], axis=1)

    def product(cols):
        got = dot(hidden[...], down_v[:, cols]).astype(BF)
        back = dot(grads[...], weights[:, cols]).astype(BF)
        for o in range(2):
            base = o * (half + cap)
            outs[base : base + cap, cols] = got[o * cap : (o + 1) * cap, :]
            outs[base + cap : base + cap + half, cols] = back[o * half : (o + 1) * half, :]

    write_chunks(product, outs, mine, other, out_sems)
    second_o[0] = ADAPTER_SCALE * dot(low_v[:, :rank], grad_gate, TN)
    second_o[1] = ADAPTER_SCALE * dot(low_v[:, rank:], grad_up, TN)

    lanes = 2 * rank
    row = lax.broadcasted_iota(jnp.int32, (lanes, lanes), 0)
    col = lax.broadcasted_iota(jnp.int32, (lanes, lanes), 1)
    members = rank // 4
    away, factor, member = row // (2 * members), (row // members) % 2, row % members
    wanted = factor * rank + (place[2] ^ away) * members + member
    order = jnp.where(wanted == col, 1.0, 0.0).astype(BF)
    straight = place[1] == 0
    for k in range(N_Y):
        ours = grad_low[k * cap : (k + 1) * cap, :].astype(F32)
        theirs = grad_low[(N_Y + k) * cap : (N_Y + k + 1) * cap, :].astype(F32)
        rows = jnp.concatenate([jnp.where(straight, ours, theirs), jnp.where(straight, theirs, ours)], axis=0)
        at = pl.multiple_of(lax.div(block_of(place, k, False), 2) * 2 * cap, 2 * cap)
        low_t[:, pl.ds(at, 2 * cap)] = dot(order, rows.astype(BF), NT).astype(BF)
    finish_chunks(outs, mine, other, out_sems)
    wait(saved)


def rest(cap, place, near, far, pre_near, gate_up, down, first, second):
    width, h, both = down.shape[1], down.shape[0], 2 * second.shape[1]
    rows = 2 * N_Y * cap
    return call(
        functools.partial(rest_kernel, cap),
        [
            shape((both, rows)),
            shape((rows, width // (2 * N_Y))),
            shape(second.shape, F32),
            shape((rows // 2 + cap, width)),
            shape((rows // 2 + cap, width)),
        ],
        [place, *near, *far, *pre_near, gate_up, down, first, second],
        [SMEM] + [HBM] * 14 + [VMEM],
        [VMEM, HBM, VMEM, HBM, HBM],
        scratch=[
            pltpu.VMEM((2 * cap, width), BF),
            pltpu.VMEM((rows, width), BF),
            pltpu.VMEM((rows, h), F32),
            pltpu.VMEM((rows, h), F32),
            pltpu.VMEM((rows, both), BF),
            pltpu.VMEM((2 * h + both, width), BF),
            pltpu.VMEM(down.shape, BF),
            pltpu.VMEM((2 * cap, h), BF),
            pltpu.VMEM((rows, 2 * h + both), BF),
            pltpu.VMEM((rows + 2 * cap, width), BF),
            pltpu.SemaphoreType.DMA((8 * N_Y + 3,)),
            pltpu.SemaphoreType.DMA((8 + 2 * N_Y,)),
        ],
        flops=10**10,
        name="rest_rows",
    )


def pack_kernel(cap, n_z, place, *refs):
    sources, outs, (own, came, packed, sems, out_sems) = refs[:4], refs[4 : 4 + N_Y], refs[4 + N_Y :]
    n = N_Y
    core, x = place[1], place[2]
    lanes = own.shape[2] // (n_z * n)
    copies = []
    for which in range(2):
        for k in range(n):
            for i, target in enumerate((own, came)):
                near, last = sources[2 * i], sources[2 * i + 1]
                if which:
                    source = last.at[pl.ds((1 + k) * cap, cap), :]
                elif k == 2:
                    source = last.at[pl.ds(0, cap), :]
                else:
                    source = near.at[pl.ds(min(k, 2) * cap, cap), :]
                to = target.at[which, pl.ds(k * cap, cap), :]
                copies.append(start(source, to, sems.at[len(copies)]))

    def block(which, i, q, z):
        cols = pl.ds(pl.multiple_of(z * n * lanes + lax.rem(x + q, n) * lanes, lanes), lanes)
        here = own[which, i * cap : (i + 1) * cap, cols].astype(F32)
        j = (n - i) % n
        return (here + came[which, j * cap : (j + 1) * cap, cols].astype(F32)).astype(BF)

    def store(which, straight):
        for to in range(n):
            for slot in range(n):
                i, q = (to, slot) if straight else (slot, to)
                at = (2 * slot + which) * cap
                for z in range(n_z):
                    packed[to, at : at + cap, z * lanes : (z + 1) * lanes] = block(which, i, q, z)
            if which:
                start(packed.at[to], outs[to], out_sems.at[to])

    for which in range(2):
        wait(copies[which * 2 * n : (which + 1) * 2 * n])

        @pl.when(core == 0)
        def _():
            store(which, True)

        @pl.when(core == 1)
        def _():
            store(which, False)

    for to in range(n):
        pltpu.make_async_copy(packed.at[to], outs[to], out_sems.at[to]).wait()


def add_and_pack(cap, sources, place):
    n, n_z = N_Y, lax.axis_size("z")
    width = sources[0].shape[1]
    return call(
        functools.partial(pack_kernel, cap, n_z),
        [shape((2 * n * cap, width // n))] * n,
        [place, *sources],
        [SMEM] + [HBM] * len(sources),
        [HBM] * n,
        scratch=[pltpu.VMEM((2, n * cap, width), BF)] * 2
        + [
            pltpu.VMEM((n, 2 * n * cap, width // n), BF),
            pltpu.SemaphoreType.DMA((4 * n,)),
            pltpu.SemaphoreType.DMA((n,)),
        ],
        limit=20,
        name="add_and_pack",
    )


def total(parts):
    out = parts[0].astype(F32)
    for part in parts[1:]:
        out = out + part.astype(F32)
    return out


def first_moves(parts):
    return [parts[0]] + [crossed(parts[s], s, 0) for s in range(1, len(parts))]


def second_moves(once, n):
    cap = once.shape[0] // n
    blocks = [once[s * cap : (s + 1) * cap] for s in range(n)]
    return [blocks[0]] + [crossed(blocks[s], s, 1) for s in range(1, n)]


def to_tokens(rows, combine):
    n_z = lax.axis_size("z")
    cap = rows[0].shape[0]
    lanes = rows[0].shape[1] // n_z
    sent = [r.astype(BF).reshape(cap, n_z, lanes).transpose(1, 0, 2) for r in rows]
    came = lax.all_to_all(jnp.concatenate(sent, axis=2), "z", 0, 0, tiled=True)
    came = came.reshape(n_z * cap, len(rows) * lanes)
    sums = dot(combine, came).astype(BF)
    return [sums[:, i * lanes : (i + 1) * lanes] for i in range(len(rows))]


def shards(
    tokens,
    routed_experts,
    choice_weights,
    gate_up_weight,
    down_weight,
    adapter_first_factors,
    adapter_second_factors,
    cotangent,
):
    n_y, n_c, n_z, n_x = (lax.axis_size(a) for a in ("y", "core", "z", "x"))
    y, core, z, x = (lax.axis_index(a) for a in ("y", "core", "z", "x"))
    tok_count, width = tokens.shape
    cap = tok_count // 2
    rank = adapter_second_factors.shape[1]
    member_cols = rank // n_x
    hidden_count = down_weight.shape[0]
    part_width = width // (n_y * n_c)
    gate_up = gate_up_weight.swapaxes(1, 2).reshape(2 * hidden_count, width)

    place = jnp.stack([y, core, x, z]).astype(jnp.int32)
    own, far_first, row_gate = expert_rows(
        tokens, cotangent, adapter_first_factors, routed_experts.T, choice_weights.T, rank, place
    )
    chosen = jnp.any(routed_experts[:, :, None] == jnp.arange(n_z, dtype=jnp.int32), axis=1)
    earlier = jnp.arange(tok_count)[:, None] > jnp.arange(tok_count)[None, :]
    placed = dot(earlier.astype(BF), chosen.astype(BF)).astype(jnp.int32)
    combine = (placed[:, :, None] == jnp.arange(cap, dtype=jnp.int32)) & chosen[:, :, None]
    combine = combine.astype(BF).reshape(tok_count, n_z * cap)

    behind = ahead(own)
    front = ahead(own, -1)
    own_s = swap(own)
    far_first = ahead(far_first, 2)
    far_first_s = swap(far_first)
    behind, front, _ = lax.optimization_barrier((behind, front, far_first_s))
    front_s = swap(behind)
    behind_s = swap(front)
    far = ahead(tie(behind[own.shape[0] - 2 * cap :], front_s, behind_s))

    weights = (gate_up, down_weight)
    near = [own, front, behind, own_s, front_s, behind_s]
    *pre_near, mine_near, other_near, first = forward(
        cap, (0, 1, 3), place, near, [far_first, far_first_s], *weights, adapter_second_factors
    )
    came_near = swap(other_near)
    far = tie(far, mine_near)
    far_s = swap(far)
    low_t, x_part, second_gradient, mine_rest, other_rest = rest(
        cap, place, near, [far, far_s], pre_near, *weights, first, adapter_second_factors
    )

    def crossing(axis, bit):
        return [(i, i ^ bit) for i in range(lax.axis_size(axis))]

    cols = low_t.shape[0] // n_x
    low_sum = low_t.astype(F32) + swap(low_t).astype(F32)
    came_rest = swap(other_rest)
    sent = low_sum[2 * cols :].astype(BF)
    moved = lax.ppermute(sent, "x", crossing("x", 2))
    parts = add_and_pack(cap, [mine_near, mine_rest, came_near, came_rest], place)
    got = first_moves(parts)
    got_again = second_moves(total(got).astype(BF), n_y)
    pair = tie(low_sum[: 2 * cols], *got) + moved.astype(F32)
    low_sum = lax.ppermute(pair[cols:].astype(BF), "x", crossing("x", 1)).astype(F32)
    low_sum = tie(pair[:cols], got_again[1]) + low_sum
    low_sum = low_sum + lax.ppermute(low_sum, "y", crossing("y", 2))
    sums = total(got_again)
    mixed, token_gradient = to_tokens([sums[:cap] * row_gate, sums[cap:]], combine)
    summed = (low_sum + lax.ppermute(low_sum, "y", crossing("y", 1))).astype(BF)
    first_gradient = dot(summed, x_part).reshape(2, member_cols, part_width).transpose(0, 2, 1)
    return (mixed, token_gradient, first_gradient, second_gradient)


def solution(mesh):
    n_y, n_x = 4, 4
    n_dp, n_et = mesh.devices.shape
    fine = Mesh(
        mesh.devices.reshape(n_y, n_dp // n_y, n_et // n_x, n_x), ("y", "core", "z", "x")
    )
    dp, et = ("y", "core"), ("z", "x")
    both = et + dp
    return jax.shard_map(
        shards,
        mesh=fine,
        in_specs=(
            P(dp, None),
            P(dp, None),
            P(dp, None),
            P(None, None, both),
            P(both, None),
            P(None, dp, None),
            P(None, None, both),
            P(dp, None),
        ),
        out_specs=(P(dp, et), P(dp, et), P(None, dp, et), P(None, None, both)),
        check_vma=False,
    )
```

```python
import functools

import jax
import jax.numpy as jnp
from jax import lax
from jax.experimental import pallas as pl
from jax.experimental.pallas import tpu as pltpu
from jax.sharding import Mesh, PartitionSpec as P

ADAPTER_SCALE = 0.5
BF = jnp.bfloat16
F32 = jnp.float32


NT = (((1,), (1,)), ((), ()))
TN = (((0,), (0,)), ((), ()))
NN = (((1,), (0,)), ((), ()))
VMEM = pl.BlockSpec(memory_space=pltpu.VMEM)
HBM = pl.BlockSpec(memory_space=pl.ANY)
SMEM = pl.BlockSpec(memory_space=pltpu.SMEM)


def dot(a, b, dims=NN):
    return lax.dot_general(a, b, dims, preferred_element_type=F32)


def shape(dims, dtype=BF):
    return jax.ShapeDtypeStruct(dims, dtype)


def call(kernel, out_shape, inputs, in_specs, out_specs, scratch=(), name=None, limit=50, flops=0):
    return pl.pallas_call(
        kernel,
        out_shape=out_shape,
        in_specs=in_specs,
        out_specs=out_specs,
        scratch_shapes=list(scratch),
        compiler_params=pltpu.CompilerParams(vmem_limit_bytes=limit * 1024 * 1024),
        cost_estimate=pl.CostEstimate(flops=flops, bytes_accessed=0, transcendentals=0),
        name=name,
    )(*inputs)


def start(source, target, sem):
    copy = pltpu.make_async_copy(source, target, sem)
    copy.start()
    return copy


def tie(value, *earlier):
    return lax.optimization_barrier((value, *earlier))[0]


def swap(values):
    return lax.ppermute(values, "core", [(0, 1), (1, 0)])


def ahead(values, step=1):
    n_y = lax.axis_size("y")
    pairs = [(2 * y + c, 2 * ((y + step * (1 - 2 * c)) % n_y) + c) for y in range(n_y) for c in range(2)]
    return lax.ppermute(values, ("y", "core"), pairs)


def crossed(values, step, first):
    n_y, n_x = lax.axis_size("y"), lax.axis_size("x")
    pairs = []
    for y in range(n_y):
        for c in range(2):
            for x in range(n_x):
                to = ((y + step * (1 - 2 * c)) % n_y, x) if c == first else (y, (x + step) % n_x)
                pairs.append(((y * 2 + c) * n_x + x, (to[0] * 2 + c) * n_x + to[1]))
    return lax.ppermute(values, ("y", "core", "x"), pairs)


def rows_kernel(
    rank, place, tokens, cotangent, first, experts, values, out_o, far_o, gate_o, tokens_v, cotangent_v, first_v, out, sems
):
    copies = [
        start(a, b, sems.at[i])
        for i, (a, b) in enumerate(((first, first_v), (tokens, tokens_v), (cotangent, cotangent_v)))
    ]
    cap, extra = gate_o.shape[0], far_o.shape[0]
    count = 2 * cap
    hits = [experts[j : j + 1, :] == place[3] for j in range(2)]
    weight = sum(jnp.where(hit, values[j : j + 1, :], 0.0) for j, hit in enumerate(hits))
    named = jnp.where(hits[0] | hits[1], 1.0, 0.0)
    before = lax.broadcasted_iota(jnp.int32, (count, count), 0) < lax.broadcasted_iota(jnp.int32, (count, count), 1)
    placed = dot(jnp.broadcast_to(named, (8, count)).astype(BF), jnp.where(before, 1.0, 0.0).astype(BF))[:1, :]
    slot = lax.broadcasted_iota(jnp.int32, (cap, count), 0)
    match = (jnp.broadcast_to(placed, (cap, count)).astype(jnp.int32) == slot) & (
        jnp.broadcast_to(named, (cap, count)) > 0.5
    )
    gate = jnp.sum(jnp.where(match, jnp.broadcast_to(weight, (cap, count)), 0.0), axis=1, keepdims=True)
    gate_o[...] = gate
    pick = jnp.where(match, 1.0, 0.0).astype(BF)
    n, cols = first.shape[1], first.shape[2]
    row = lax.broadcasted_iota(jnp.int32, (2 * rank, cols), 0)
    col = lax.broadcasted_iota(jnp.int32, (2 * rank, cols), 1)
    copies[0].wait()
    held = None
    for m in range(2):
        take = (col == place[3] * rank + row - m * rank) & (row >= m * rank) & (row < (m + 1) * rank)
        term = dot(jnp.where(take, 1.0, 0.0).astype(BF), first_v[m], NT)
        held = term if held is None else held + term
    held = held.astype(BF)
    for j in range(2 * rank // extra):
        piece = held[j * extra : (j + 1) * extra, :]
        out[:extra, j * n : (j + 1) * n] = piece
    far_copy = start(out.at[pl.ds(0, extra), :], far_o, sems.at[3])
    copies[1].wait()
    out[extra : extra + cap, :] = dot(pick, tokens_v[...]).astype(BF)
    copies[2].wait()
    out[cap + extra :, :] = (dot(pick, cotangent_v[...]) * gate).astype(BF)
    start(out, out_o, sems.at[4]).wait()
    far_copy.wait()


def expert_rows(tokens, cotangent, first, experts, values, rank, place):
    count, width = tokens.shape
    cap = count // 2
    extra = first.shape[1] * 2 * rank // width
    return call(
        functools.partial(rows_kernel, rank),
        [shape((2 * cap + extra, width)), shape((extra, width)), shape((cap, 1), F32)],
        [place, tokens, cotangent, first, experts, values],
        [SMEM, HBM, HBM, HBM, VMEM, VMEM],
        [HBM, HBM, VMEM],
        scratch=[
            pltpu.VMEM(tokens.shape, BF),
            pltpu.VMEM(cotangent.shape, BF),
            pltpu.VMEM(first.shape, BF),
            pltpu.VMEM((2 * cap + extra, width), BF),
            pltpu.SemaphoreType.DMA((5,)),
        ],
        limit=60,
        name="expert_rows",
    )


N_Y = 4
CHUNK = 2048


def block_of(place, k, other):
    y, core = place[0], place[1]
    way = 1 - 2 * core
    return lax.rem(y + way * k + 2 * N_Y, N_Y) * 2 + (1 - core if other else core)


def wait(copies):
    for c in copies:
        c.wait()


def chunk_copies(i, outs, mine, other, sems):
    cols = pl.ds(pl.multiple_of(i * CHUNK, CHUNK), CHUNK)
    half = mine.shape[0]
    return [
        pltpu.make_async_copy(outs.at[pl.ds(half, half), cols], other.at[:, cols], sems.at[2 * i]),
        pltpu.make_async_copy(outs.at[pl.ds(0, half), cols], mine.at[:, cols], sems.at[2 * i + 1]),
    ]


def write_chunks(product, outs, mine, other, sems):
    def step(i, carry):
        product(pl.ds(pl.multiple_of(i * CHUNK, CHUNK), CHUNK))
        for c in chunk_copies(i, outs, mine, other, sems):
            c.start()
        return carry

    lax.fori_loop(0, outs.shape[1] // CHUNK, step, 0)


def finish_chunks(outs, mine, other, sems):
    def step(i, carry):
        wait(chunk_copies(i, outs, mine, other, sems))
        return carry

    lax.fori_loop(0, outs.shape[1] // CHUNK, step, 0)


def fetch_columns(fetch, source, target, parts=4):
    rows, step = source.shape[0], source.shape[1] // parts
    cols = [pl.ds(i * step, step) for i in range(parts)]
    return [fetch(source.at[:, c], target.at[pl.ds(0, rows), c]) for c in cols]


def preactivations(xs, weights, second, arrivals):
    h, rank = second.shape[2], second.shape[1]
    step = xs.shape[1] // len(arrivals)
    pre = None
    for i, arrival in enumerate(arrivals):
        arrival.wait()
        cols = slice(i * step, (i + 1) * step)
        term = dot(xs[:, cols], weights[:, cols], NT)
        pre = term if pre is None else pre + term
    low = pre[:, 2 * h :].astype(BF)
    gate = pre[:, :h] + ADAPTER_SCALE * dot(low[:, :rank], second[0])
    up = pre[:, h : 2 * h] + ADAPTER_SCALE * dot(low[:, rank:], second[1])
    return gate, up, low, (gate / (1.0 + jnp.exp(-gate)) * up).astype(BF)


def forward_kernel(cap, steps, place, *refs):
    n = 2 * len(steps)
    blocks, fars, (gate_up, down, second), refs = refs[:n], refs[n : n + 2], refs[n + 2 : n + 5], refs[n + 5 :]
    (gate_o, up_o, low_o, mine, other, first_out), refs = refs[:6], refs[6:]
    xs, weights, down_v, hidden, gate_v, up_v, low_v, packed, outs, in_sems, out_sems = refs
    h, rank, width = down.shape[0], second.shape[1], down.shape[1]
    lanes, extra = 2 * rank, fars[0].shape[0]
    first = weights.at[pl.ds(2 * h, lanes), :]
    count = iter(range(64))

    def fetch(source, target):
        return start(source, target, in_sems.at[next(count)])

    sources = [b.at[pl.ds(0, extra), :] for b in blocks] + list(fars)
    got_first = [fetch(a, packed.at[pl.ds(i * extra, extra), :]) for i, a in enumerate(sources)]
    got_x = [fetch(b.at[pl.ds(extra, cap), :], xs.at[pl.ds(i * cap, cap), :]) for i, b in enumerate(blocks)]
    got_gate_up = fetch_columns(fetch, gate_up, weights)
    got_down = fetch(down, down_v)

    wait(got_first)
    step = extra * width // lanes
    held = [(k, o) for o in (False, True) for k in steps] + [(2, False), (2, True)]
    for i, (k, o) in enumerate(held):
        at = pl.ds(pl.multiple_of(block_of(place, k, o) * step, step), step)
        for j in range(lanes // extra):
            piece = packed[i * extra : (i + 1) * extra, j * step : (j + 1) * step]
            weights[2 * h + j * extra : 2 * h + (j + 1) * extra, at] = piece
    save = [start(first, first_out, out_sems.at[8])]
    wait(got_x)
    gate, up, low, act = preactivations(xs, weights, second, got_gate_up)
    gate_v[...] = gate
    up_v[...] = up
    low_v[...] = low
    hidden[...] = act
    for i, (a, b) in enumerate(((gate_v, gate_o), (up_v, up_o), (low_v, low_o))):
        save.append(start(a, b, out_sems.at[9 + i]))
    got_down.wait()

    def product(cols):
        outs[:, cols] = dot(hidden[...], down_v[:, cols]).astype(BF)

    write_chunks(product, outs, mine, other, out_sems)
    finish_chunks(outs, mine, other, out_sems)
    wait(save)


def forward(cap, steps, place, blocks, fars, gate_up, down, second):
    n, width, h, both = len(blocks), down.shape[1], down.shape[0], 2 * second.shape[1]
    rows = n * cap
    return call(
        functools.partial(forward_kernel, cap, steps),
        [
            shape((rows, h), F32),
            shape((rows, h), F32),
            shape((rows, both)),
            shape((rows // 2, width)),
            shape((rows // 2, width)),
            shape((both, width)),
        ],
        [place, *blocks, *fars, gate_up, down, second],
        [SMEM] + [HBM] * (n + 4) + [VMEM],
        [HBM] * 6,
        scratch=[
            pltpu.VMEM((rows, width), BF),
            pltpu.VMEM((2 * h + both, width), BF),
            pltpu.VMEM(down.shape, BF),
            pltpu.VMEM((rows, h), BF),
            pltpu.VMEM((rows, h), F32),
            pltpu.VMEM((rows, h), F32),
            pltpu.VMEM((rows, both), BF),
            pltpu.VMEM(((n + 2) * fars[0].shape[0], width), BF),
            pltpu.VMEM((rows, width), BF),
            pltpu.SemaphoreType.DMA((2 * n + 8,)),
            pltpu.SemaphoreType.DMA((12,)),
        ],
        flops=10**10,
        name="forward_rows",
    )


def rest_kernel(cap, place, *refs):
    near, far, refs = refs[:6], refs[6:8], refs[8:]
    (gate_n, up_n, low_n, gate_up, down, first, second), refs = refs[:7], refs[7:]
    (low_t, part, second_o, mine, other), refs = refs[:5], refs[5:]
    xs, ds, gate_v, up_v, low_v, weights, down_v, hidden, grads, outs, in_sems, out_sems = refs
    h, rank, width = down.shape[0], second.shape[1], down.shape[1]
    n = 2 * N_Y
    half = N_Y * cap
    count = iter(range(64))

    def fetch(source, target):
        return start(source, target, in_sems.at[next(count)])

    def rows_of(i):
        return pl.ds(i * cap, cap)

    place_of = {}
    for o in range(2):
        for j, k in enumerate((0, 1, 3)):
            place_of[o * N_Y + k] = (False, 3 * o + j)
        place_of[o * N_Y + 2] = (True, o)
    extra = near[0].shape[0] - 2 * cap
    got_x = [fetch(far[o].at[pl.ds(0, cap), :], xs.at[rows_of(o), :]) for o in range(2)]
    got_first = fetch(first, weights.at[pl.ds(2 * h, 2 * rank), :])
    got_gate_up = fetch_columns(fetch, gate_up, weights)
    got_down = fetch(down, down_v)
    got_d, got_pre, saved = [], [], []
    for i in range(n):
        is_far, j = place_of[i]
        source = far[j].at[pl.ds(cap, cap), :] if is_far else near[j].at[pl.ds(extra + cap, cap), :]
        got_d.append(fetch(source, ds.at[rows_of(i), :]))
    for i in range(n):
        is_far, j = place_of[i]
        if not is_far:
            for source, target in ((gate_n, gate_v), (up_n, up_v), (low_n, low_v)):
                got_pre.append(fetch(source.at[rows_of(j), :], target.at[rows_of(i), :]))
    step = part.shape[1]
    cols = pl.ds(pl.multiple_of((place[0] * 2 + place[1]) * step, step), step)
    for i in range(n):
        is_far, j = place_of[i]
        at = pl.multiple_of(block_of(place, i % N_Y, i >= N_Y) * cap, cap)
        source = far[j].at[pl.ds(0, cap), cols] if is_far else near[j].at[pl.ds(extra, cap), cols]
        saved.append(start(source, part.at[pl.ds(at, cap), :], out_sems.at[8 + i]))

    wait(got_x)
    got_first.wait()
    gate, up, low, act = preactivations(xs, weights, second, got_gate_up)
    hidden[...] = act
    for o in range(2):
        to = (o * N_Y + 2) * cap
        for value, target in ((gate, gate_v), (up, up_v), (low, low_v)):
            target[to : to + cap, :] = value[o * cap : (o + 1) * cap, :]

    got_down.wait()
    wait(got_d)
    grad = dot(ds[...], down_v[...], NT)
    wait(got_pre)
    gate, up = gate_v[...], up_v[...]
    sig = 1.0 / (1.0 + jnp.exp(-gate))
    grad_gate = (grad * up * sig * (1.0 + gate * (1.0 - sig))).astype(BF)
    grad_up = (grad * gate * sig).astype(BF)
    both = [ADAPTER_SCALE * dot(grad_gate, second[0], NT), ADAPTER_SCALE * dot(grad_up, second[1], NT)]
    grad_low = jnp.concatenate(both, axis=1).astype(BF)
    grads[...] = jnp.concatenate([grad_gate, grad_up, grad_low], axis=1)

    def product(cols):
        got = dot(hidden[...], down_v[:, cols]).astype(BF)
        back = dot(grads[...], weights[:, cols]).astype(BF)
        for o in range(2):
            base = o * (half + cap)
            outs[base : base + cap, cols] = got[o * cap : (o + 1) * cap, :]
            outs[base + cap : base + cap + half, cols] = back[o * half : (o + 1) * half, :]

    write_chunks(product, outs, mine, other, out_sems)
    second_o[0] = ADAPTER_SCALE * dot(low_v[:, :rank], grad_gate, TN)
    second_o[1] = ADAPTER_SCALE * dot(low_v[:, rank:], grad_up, TN)

    lanes = 2 * rank
    row = lax.broadcasted_iota(jnp.int32, (lanes, lanes), 0)
    col = lax.broadcasted_iota(jnp.int32, (lanes, lanes), 1)
    members = rank // 4
    away, factor, member = row // (2 * members), (row // members) % 2, row % members
    wanted = factor * rank + (place[2] ^ away) * members + member
    order = jnp.where(wanted == col, 1.0, 0.0).astype(BF)
    straight = place[1] == 0
    for k in range(N_Y):
        ours = grad_low[k * cap : (k + 1) * cap, :].astype(F32)
        theirs = grad_low[(N_Y + k) * cap : (N_Y + k + 1) * cap, :].astype(F32)
        rows = jnp.concatenate([jnp.where(straight, ours, theirs), jnp.where(straight, theirs, ours)], axis=0)
        at = pl.multiple_of(lax.div(block_of(place, k, False), 2) * 2 * cap, 2 * cap)
        low_t[:, pl.ds(at, 2 * cap)] = dot(order, rows.astype(BF), NT).astype(BF)
    finish_chunks(outs, mine, other, out_sems)
    wait(saved)


def rest(cap, place, near, far, pre_near, gate_up, down, first, second):
    width, h, both = down.shape[1], down.shape[0], 2 * second.shape[1]
    rows = 2 * N_Y * cap
    return call(
        functools.partial(rest_kernel, cap),
        [
            shape((both, rows)),
            shape((rows, width // (2 * N_Y))),
            shape(second.shape, F32),
            shape((rows // 2 + cap, width)),
            shape((rows // 2 + cap, width)),
        ],
        [place, *near, *far, *pre_near, gate_up, down, first, second],
        [SMEM] + [HBM] * 14 + [VMEM],
        [VMEM, HBM, VMEM, HBM, HBM],
        scratch=[
            pltpu.VMEM((2 * cap, width), BF),
            pltpu.VMEM((rows, width), BF),
            pltpu.VMEM((rows, h), F32),
            pltpu.VMEM((rows, h), F32),
            pltpu.VMEM((rows, both), BF),
            pltpu.VMEM((2 * h + both, width), BF),
            pltpu.VMEM(down.shape, BF),
            pltpu.VMEM((2 * cap, h), BF),
            pltpu.VMEM((rows, 2 * h + both), BF),
            pltpu.VMEM((rows + 2 * cap, width), BF),
            pltpu.SemaphoreType.DMA((8 * N_Y + 3,)),
            pltpu.SemaphoreType.DMA((8 + 2 * N_Y,)),
        ],
        flops=10**10,
        name="rest_rows",
    )


def pack_kernel(cap, n_z, place, *refs):
    sources, outs, (own, came, packed, sems, out_sems) = refs[:4], refs[4 : 4 + N_Y], refs[4 + N_Y :]
    n = N_Y
    core, x = place[1], place[2]
    lanes = own.shape[2] // (n_z * n)
    copies = []
    for which in range(2):
        for k in range(n):
            for i, target in enumerate((own, came)):
                near, last = sources[2 * i], sources[2 * i + 1]
                if which:
                    source = last.at[pl.ds((1 + k) * cap, cap), :]
                elif k == 2:
                    source = last.at[pl.ds(0, cap), :]
                else:
                    source = near.at[pl.ds(min(k, 2) * cap, cap), :]
                to = target.at[which, pl.ds(k * cap, cap), :]
                copies.append(start(source, to, sems.at[len(copies)]))

    def block(which, i, q, z):
        cols = pl.ds(pl.multiple_of(z * n * lanes + lax.rem(x + q, n) * lanes, lanes), lanes)
        here = own[which, i * cap : (i + 1) * cap, cols].astype(F32)
        j = (n - i) % n
        return (here + came[which, j * cap : (j + 1) * cap, cols].astype(F32)).astype(BF)

    def store(which, straight):
        for to in range(n):
            for slot in range(n):
                i, q = (to, slot) if straight else (slot, to)
                at = (2 * slot + which) * cap
                for z in range(n_z):
                    packed[to, at : at + cap, z * lanes : (z + 1) * lanes] = block(which, i, q, z)
            if which:
                start(packed.at[to], outs[to], out_sems.at[to])

    for which in range(2):
        wait(copies[which * 2 * n : (which + 1) * 2 * n])

        @pl.when(core == 0)
        def _():
            store(which, True)

        @pl.when(core == 1)
        def _():
            store(which, False)

    for to in range(n):
        pltpu.make_async_copy(packed.at[to], outs[to], out_sems.at[to]).wait()


def add_and_pack(cap, sources, place):
    n, n_z = N_Y, lax.axis_size("z")
    width = sources[0].shape[1]
    return call(
        functools.partial(pack_kernel, cap, n_z),
        [shape((2 * n * cap, width // n))] * n,
        [place, *sources],
        [SMEM] + [HBM] * len(sources),
        [HBM] * n,
        scratch=[pltpu.VMEM((2, n * cap, width), BF)] * 2
        + [
            pltpu.VMEM((n, 2 * n * cap, width // n), BF),
            pltpu.SemaphoreType.DMA((4 * n,)),
            pltpu.SemaphoreType.DMA((n,)),
        ],
        limit=20,
        name="add_and_pack",
    )


def total(parts):
    out = parts[0].astype(F32)
    for part in parts[1:]:
        out = out + part.astype(F32)
    return out


def first_moves(parts):
    return [parts[0]] + [crossed(parts[s], s, 0) for s in (2, 1, 3)]


def second_moves(once, n):
    cap = once.shape[0] // n
    blocks = [once[s * cap : (s + 1) * cap] for s in range(n)]
    return [blocks[0]] + [crossed(blocks[s], s, 1) for s in range(1, n)]


def to_tokens(rows, combine):
    n_z = lax.axis_size("z")
    cap = rows[0].shape[0]
    lanes = rows[0].shape[1] // n_z
    sent = [r.astype(BF).reshape(cap, n_z, lanes).transpose(1, 0, 2) for r in rows]
    came = lax.all_to_all(jnp.concatenate(sent, axis=2), "z", 0, 0, tiled=True)
    came = came.reshape(n_z * cap, len(rows) * lanes)
    sums = dot(combine, came).astype(BF)
    return [sums[:, i * lanes : (i + 1) * lanes] for i in range(len(rows))]


def shards(
    tokens,
    routed_experts,
    choice_weights,
    gate_up_weight,
    down_weight,
    adapter_first_factors,
    adapter_second_factors,
    cotangent,
):
    n_y, n_c, n_z, n_x = (lax.axis_size(a) for a in ("y", "core", "z", "x"))
    y, core, z, x = (lax.axis_index(a) for a in ("y", "core", "z", "x"))
    tok_count, width = tokens.shape
    cap = tok_count // 2
    rank = adapter_second_factors.shape[1]
    member_cols = rank // n_x
    hidden_count = down_weight.shape[0]
    part_width = width // (n_y * n_c)
    gate_up = gate_up_weight.swapaxes(1, 2).reshape(2 * hidden_count, width)

    place = jnp.stack([y, core, x, z]).astype(jnp.int32)
    own, far_first, row_gate = expert_rows(
        tokens, cotangent, adapter_first_factors, routed_experts.T, choice_weights.T, rank, place
    )
    chosen = jnp.any(routed_experts[:, :, None] == jnp.arange(n_z, dtype=jnp.int32), axis=1)
    earlier = jnp.arange(tok_count)[:, None] > jnp.arange(tok_count)[None, :]
    placed = dot(earlier.astype(BF), chosen.astype(BF)).astype(jnp.int32)
    combine = (placed[:, :, None] == jnp.arange(cap, dtype=jnp.int32)) & chosen[:, :, None]
    combine = combine.astype(BF).reshape(tok_count, n_z * cap)

    behind = ahead(own)
    front = ahead(own, -1)
    own_s = swap(own)
    far_first = ahead(far_first, 2)
    far_first_s = swap(far_first)
    behind, front, _ = lax.optimization_barrier((behind, front, far_first_s))
    front_s = swap(behind)
    behind_s = swap(front)
    far = ahead(tie(behind[own.shape[0] - 2 * cap :], front_s, behind_s))

    weights = (gate_up, down_weight)
    near = [own, front, behind, own_s, front_s, behind_s]
    *pre_near, mine_near, other_near, first = forward(
        cap, (0, 1, 3), place, near, [far_first, far_first_s], *weights, adapter_second_factors
    )
    came_near = swap(other_near)
    far = tie(far, mine_near)
    far_s = swap(far)
    low_t, x_part, second_gradient, mine_rest, other_rest = rest(
        cap, place, near, [far, far_s], pre_near, *weights, first, adapter_second_factors
    )

    def crossing(axis, bit):
        return [(i, i ^ bit) for i in range(lax.axis_size(axis))]

    cols = low_t.shape[0] // n_x
    low_sum = low_t.astype(F32) + swap(low_t).astype(F32)
    came_rest = swap(other_rest)
    sent = low_sum[2 * cols :].astype(BF)
    moved = lax.ppermute(sent, "x", crossing("x", 2))
    parts = add_and_pack(cap, [mine_near, mine_rest, came_near, came_rest], place)
    got = first_moves(parts)
    got_again = second_moves(total(got).astype(BF), n_y)
    pair = tie(low_sum[: 2 * cols], *got) + moved.astype(F32)
    low_sum = lax.ppermute(pair[cols:].astype(BF), "x", crossing("x", 1)).astype(F32)
    low_sum = tie(pair[:cols], got_again[1]) + low_sum
    low_sum = low_sum + lax.ppermute(low_sum, "y", crossing("y", 2))
    sums = total(got_again)
    mixed, token_gradient = to_tokens([sums[:cap] * row_gate, sums[cap:]], combine)
    summed = (low_sum + lax.ppermute(low_sum, "y", crossing("y", 1))).astype(BF)
    first_gradient = dot(summed, x_part).reshape(2, member_cols, part_width).transpose(0, 2, 1)
    return (mixed, token_gradient, first_gradient, second_gradient)


def solution(mesh):
    n_y, n_x = 4, 4
    n_dp, n_et = mesh.devices.shape
    fine = Mesh(
        mesh.devices.reshape(n_y, n_dp // n_y, n_et // n_x, n_x), ("y", "core", "z", "x")
    )
    dp, et = ("y", "core"), ("z", "x")
    both = et + dp
    return jax.shard_map(
        shards,
        mesh=fine,
        in_specs=(
            P(dp, None),
            P(dp, None),
            P(dp, None),
            P(None, None, both),
            P(both, None),
            P(None, dp, None),
            P(None, None, both),
            P(dp, None),
        ),
        out_specs=(P(dp, et), P(dp, et), P(None, dp, et), P(None, None, both)),
        check_vma=False,
    )
```

```python
import functools

import jax
import jax.numpy as jnp
from jax import lax
from jax.experimental import pallas as pl
from jax.experimental.pallas import tpu as pltpu
from jax.sharding import Mesh, PartitionSpec as P

ADAPTER_SCALE = 0.5
BF = jnp.bfloat16
F32 = jnp.float32


NT = (((1,), (1,)), ((), ()))
TN = (((0,), (0,)), ((), ()))
NN = (((1,), (0,)), ((), ()))
VMEM = pl.BlockSpec(memory_space=pltpu.VMEM)
HBM = pl.BlockSpec(memory_space=pl.ANY)
SMEM = pl.BlockSpec(memory_space=pltpu.SMEM)


def dot(a, b, dims=NN):
    return lax.dot_general(a, b, dims, preferred_element_type=F32)


def shape(dims, dtype=BF):
    return jax.ShapeDtypeStruct(dims, dtype)


def call(kernel, out_shape, inputs, in_specs, out_specs, scratch=(), name=None, limit=50, flops=0):
    return pl.pallas_call(
        kernel,
        out_shape=out_shape,
        in_specs=in_specs,
        out_specs=out_specs,
        scratch_shapes=list(scratch),
        compiler_params=pltpu.CompilerParams(vmem_limit_bytes=limit * 1024 * 1024),
        cost_estimate=pl.CostEstimate(flops=flops, bytes_accessed=0, transcendentals=0),
        name=name,
    )(*inputs)


def start(source, target, sem):
    copy = pltpu.make_async_copy(source, target, sem)
    copy.start()
    return copy


def tie(value, *earlier):
    return lax.optimization_barrier((value, *earlier))[0]


def swap(values):
    return lax.ppermute(values, "core", [(0, 1), (1, 0)])


def ahead(values, step=1):
    n_y = lax.axis_size("y")
    pairs = [(2 * y + c, 2 * ((y + step * (1 - 2 * c)) % n_y) + c) for y in range(n_y) for c in range(2)]
    return lax.ppermute(values, ("y", "core"), pairs)


def crossed(values, step, first):
    n_y, n_x = lax.axis_size("y"), lax.axis_size("x")
    pairs = []
    for y in range(n_y):
        for c in range(2):
            for x in range(n_x):
                to = ((y + step * (1 - 2 * c)) % n_y, x) if c == first else (y, (x + step) % n_x)
                pairs.append(((y * 2 + c) * n_x + x, (to[0] * 2 + c) * n_x + to[1]))
    return lax.ppermute(values, ("y", "core", "x"), pairs)


def rows_kernel(
    rank, place, tokens, cotangent, first, experts, values, out_o, far_o, gate_o, tokens_v, cotangent_v, first_v, out, sems
):
    copies = [
        start(a, b, sems.at[i])
        for i, (a, b) in enumerate(((first, first_v), (tokens, tokens_v), (cotangent, cotangent_v)))
    ]
    cap, extra = gate_o.shape[0], far_o.shape[0]
    count = 2 * cap
    hits = [experts[j : j + 1, :] == place[3] for j in range(2)]
    weight = sum(jnp.where(hit, values[j : j + 1, :], 0.0) for j, hit in enumerate(hits))
    named = jnp.where(hits[0] | hits[1], 1.0, 0.0)
    before = lax.broadcasted_iota(jnp.int32, (count, count), 0) < lax.broadcasted_iota(jnp.int32, (count, count), 1)
    placed = dot(jnp.broadcast_to(named, (8, count)).astype(BF), jnp.where(before, 1.0, 0.0).astype(BF))[:1, :]
    slot = lax.broadcasted_iota(jnp.int32, (cap, count), 0)
    match = (jnp.broadcast_to(placed, (cap, count)).astype(jnp.int32) == slot) & (
        jnp.broadcast_to(named, (cap, count)) > 0.5
    )
    gate = jnp.sum(jnp.where(match, jnp.broadcast_to(weight, (cap, count)), 0.0), axis=1, keepdims=True)
    gate_o[...] = gate
    pick = jnp.where(match, 1.0, 0.0).astype(BF)
    n, cols = first.shape[1], first.shape[2]
    row = lax.broadcasted_iota(jnp.int32, (2 * rank, cols), 0)
    col = lax.broadcasted_iota(jnp.int32, (2 * rank, cols), 1)
    copies[0].wait()
    held = None
    for m in range(2):
        take = (col == place[3] * rank + row - m * rank) & (row >= m * rank) & (row < (m + 1) * rank)
        term = dot(jnp.where(take, 1.0, 0.0).astype(BF), first_v[m], NT)
        held = term if held is None else held + term
    held = held.astype(BF)
    for j in range(2 * rank // extra):
        piece = held[j * extra : (j + 1) * extra, :]
        out[:extra, j * n : (j + 1) * n] = piece
    far_copy = start(out.at[pl.ds(0, extra), :], far_o, sems.at[3])
    copies[1].wait()
    out[extra : extra + cap, :] = dot(pick, tokens_v[...]).astype(BF)
    copies[2].wait()
    out[cap + extra :, :] = (dot(pick, cotangent_v[...]) * gate).astype(BF)
    start(out, out_o, sems.at[4]).wait()
    far_copy.wait()


def expert_rows(tokens, cotangent, first, experts, values, rank, place):
    count, width = tokens.shape
    cap = count // 2
    extra = first.shape[1] * 2 * rank // width
    return call(
        functools.partial(rows_kernel, rank),
        [shape((2 * cap + extra, width)), shape((extra, width)), shape((cap, 1), F32)],
        [place, tokens, cotangent, first, experts, values],
        [SMEM, HBM, HBM, HBM, VMEM, VMEM],
        [HBM, HBM, VMEM],
        scratch=[
            pltpu.VMEM(tokens.shape, BF),
            pltpu.VMEM(cotangent.shape, BF),
            pltpu.VMEM(first.shape, BF),
            pltpu.VMEM((2 * cap + extra, width), BF),
            pltpu.SemaphoreType.DMA((5,)),
        ],
        limit=60,
        name="expert_rows",
    )


N_Y = 4
CHUNK = 2048


def block_of(place, k, other):
    y, core = place[0], place[1]
    way = 1 - 2 * core
    return lax.rem(y + way * k + 2 * N_Y, N_Y) * 2 + (1 - core if other else core)


def wait(copies):
    for c in copies:
        c.wait()


def chunk_copies(i, outs, mine, other, sems):
    cols = pl.ds(pl.multiple_of(i * CHUNK, CHUNK), CHUNK)
    half = mine.shape[0]
    return [
        pltpu.make_async_copy(outs.at[pl.ds(half, half), cols], other.at[:, cols], sems.at[2 * i]),
        pltpu.make_async_copy(outs.at[pl.ds(0, half), cols], mine.at[:, cols], sems.at[2 * i + 1]),
    ]


def write_chunks(product, outs, mine, other, sems):
    def step(i, carry):
        product(pl.ds(pl.multiple_of(i * CHUNK, CHUNK), CHUNK))
        for c in chunk_copies(i, outs, mine, other, sems):
            c.start()
        return carry

    lax.fori_loop(0, outs.shape[1] // CHUNK, step, 0)


def finish_chunks(outs, mine, other, sems):
    def step(i, carry):
        wait(chunk_copies(i, outs, mine, other, sems))
        return carry

    lax.fori_loop(0, outs.shape[1] // CHUNK, step, 0)


def fetch_columns(fetch, source, target, parts=4):
    rows, step = source.shape[0], source.shape[1] // parts
    cols = [pl.ds(i * step, step) for i in range(parts)]
    return [fetch(source.at[:, c], target.at[pl.ds(0, rows), c]) for c in cols]


def preactivations(xs, weights, second, arrivals):
    h, rank = second.shape[2], second.shape[1]
    step = xs.shape[1] // len(arrivals)
    pre = None
    for i, arrival in enumerate(arrivals):
        arrival.wait()
        cols = slice(i * step, (i + 1) * step)
        term = dot(xs[:, cols], weights[:, cols], NT)
        pre = term if pre is None else pre + term
    low = pre[:, 2 * h :].astype(BF)
    gate = pre[:, :h] + ADAPTER_SCALE * dot(low[:, :rank], second[0])
    up = pre[:, h : 2 * h] + ADAPTER_SCALE * dot(low[:, rank:], second[1])
    return gate, up, low, (gate / (1.0 + jnp.exp(-gate)) * up).astype(BF)


def forward_kernel(cap, steps, place, *refs):
    n = 2 * len(steps)
    blocks, fars, (gate_up, down, second), refs = refs[:n], refs[n : n + 2], refs[n + 2 : n + 5], refs[n + 5 :]
    (gate_o, up_o, low_o, mine, other, first_out), refs = refs[:6], refs[6:]
    xs, weights, down_v, hidden, gate_v, up_v, low_v, packed, outs, in_sems, out_sems = refs
    h, rank, width = down.shape[0], second.shape[1], down.shape[1]
    lanes, extra = 2 * rank, fars[0].shape[0]
    first = weights.at[pl.ds(2 * h, lanes), :]
    count = iter(range(64))

    def fetch(source, target):
        return start(source, target, in_sems.at[next(count)])

    sources = [b.at[pl.ds(0, extra), :] for b in blocks] + list(fars)
    got_first = [fetch(a, packed.at[pl.ds(i * extra, extra), :]) for i, a in enumerate(sources)]
    got_x = [fetch(b.at[pl.ds(extra, cap), :], xs.at[pl.ds(i * cap, cap), :]) for i, b in enumerate(blocks)]
    got_gate_up = fetch_columns(fetch, gate_up, weights)
    got_down = fetch(down, down_v)

    wait(got_first)
    step = extra * width // lanes
    held = [(k, o) for o in (False, True) for k in steps] + [(2, False), (2, True)]
    for i, (k, o) in enumerate(held):
        at = pl.ds(pl.multiple_of(block_of(place, k, o) * step, step), step)
        for j in range(lanes // extra):
            piece = packed[i * extra : (i + 1) * extra, j * step : (j + 1) * step]
            weights[2 * h + j * extra : 2 * h + (j + 1) * extra, at] = piece
    save = [start(first, first_out, out_sems.at[8])]
    wait(got_x)
    gate, up, low, act = preactivations(xs, weights, second, got_gate_up)
    gate_v[...] = gate
    up_v[...] = up
    low_v[...] = low
    hidden[...] = act
    for i, (a, b) in enumerate(((gate_v, gate_o), (up_v, up_o), (low_v, low_o))):
        save.append(start(a, b, out_sems.at[9 + i]))
    got_down.wait()

    def product(cols):
        outs[:, cols] = dot(hidden[...], down_v[:, cols]).astype(BF)

    write_chunks(product, outs, mine, other, out_sems)
    finish_chunks(outs, mine, other, out_sems)
    wait(save)


def forward(cap, steps, place, blocks, fars, gate_up, down, second):
    n, width, h, both = len(blocks), down.shape[1], down.shape[0], 2 * second.shape[1]
    rows = n * cap
    return call(
        functools.partial(forward_kernel, cap, steps),
        [
            shape((rows, h), F32),
            shape((rows, h), F32),
            shape((rows, both)),
            shape((rows // 2, width)),
            shape((rows // 2, width)),
            shape((both, width)),
        ],
        [place, *blocks, *fars, gate_up, down, second],
        [SMEM] + [HBM] * (n + 4) + [VMEM],
        [HBM] * 6,
        scratch=[
            pltpu.VMEM((rows, width), BF),
            pltpu.VMEM((2 * h + both, width), BF),
            pltpu.VMEM(down.shape, BF),
            pltpu.VMEM((rows, h), BF),
            pltpu.VMEM((rows, h), F32),
            pltpu.VMEM((rows, h), F32),
            pltpu.VMEM((rows, both), BF),
            pltpu.VMEM(((n + 2) * fars[0].shape[0], width), BF),
            pltpu.VMEM((rows, width), BF),
            pltpu.SemaphoreType.DMA((2 * n + 8,)),
            pltpu.SemaphoreType.DMA((12,)),
        ],
        flops=10**10,
        name="forward_rows",
    )


def rest_kernel(cap, place, *refs):
    near, far, refs = refs[:6], refs[6:8], refs[8:]
    (gate_n, up_n, low_n, gate_up, down, first, second), refs = refs[:7], refs[7:]
    (low_t, part, second_o, mine, other), refs = refs[:5], refs[5:]
    xs, ds, gate_v, up_v, low_v, weights, down_v, hidden, grads, outs, in_sems, out_sems = refs
    h, rank, width = down.shape[0], second.shape[1], down.shape[1]
    n = 2 * N_Y
    half = N_Y * cap
    count = iter(range(64))

    def fetch(source, target):
        return start(source, target, in_sems.at[next(count)])

    def rows_of(i):
        return pl.ds(i * cap, cap)

    place_of = {}
    for o in range(2):
        for j, k in enumerate((0, 1, 3)):
            place_of[o * N_Y + k] = (False, 3 * o + j)
        place_of[o * N_Y + 2] = (True, o)
    extra = near[0].shape[0] - 2 * cap
    got_x = [fetch(far[o].at[pl.ds(0, cap), :], xs.at[rows_of(o), :]) for o in range(2)]
    got_first = fetch(first, weights.at[pl.ds(2 * h, 2 * rank), :])
    got_gate_up = fetch_columns(fetch, gate_up, weights)
    got_down = fetch(down, down_v)
    got_d, got_pre, saved = [], [], []
    for i in range(n):
        is_far, j = place_of[i]
        source = far[j].at[pl.ds(cap, cap), :] if is_far else near[j].at[pl.ds(extra + cap, cap), :]
        got_d.append(fetch(source, ds.at[rows_of(i), :]))
    for i in range(n):
        is_far, j = place_of[i]
        if not is_far:
            for source, target in ((gate_n, gate_v), (up_n, up_v), (low_n, low_v)):
                got_pre.append(fetch(source.at[rows_of(j), :], target.at[rows_of(i), :]))
    step = part.shape[1]
    cols = pl.ds(pl.multiple_of((place[0] * 2 + place[1]) * step, step), step)
    for i in range(n):
        is_far, j = place_of[i]
        at = pl.multiple_of(block_of(place, i % N_Y, i >= N_Y) * cap, cap)
        source = far[j].at[pl.ds(0, cap), cols] if is_far else near[j].at[pl.ds(extra, cap), cols]
        saved.append(start(source, part.at[pl.ds(at, cap), :], out_sems.at[8 + i]))

    wait(got_x)
    got_first.wait()
    gate, up, low, act = preactivations(xs, weights, second, got_gate_up)
    hidden[...] = act
    for o in range(2):
        to = (o * N_Y + 2) * cap
        for value, target in ((gate, gate_v), (up, up_v), (low, low_v)):
            target[to : to + cap, :] = value[o * cap : (o + 1) * cap, :]

    got_down.wait()
    wait(got_d)
    grad = dot(ds[...], down_v[...], NT)
    wait(got_pre)
    gate, up = gate_v[...], up_v[...]
    sig = 1.0 / (1.0 + jnp.exp(-gate))
    grad_gate = (grad * up * sig * (1.0 + gate * (1.0 - sig))).astype(BF)
    grad_up = (grad * gate * sig).astype(BF)
    both = [ADAPTER_SCALE * dot(grad_gate, second[0], NT), ADAPTER_SCALE * dot(grad_up, second[1], NT)]
    grad_low = jnp.concatenate(both, axis=1).astype(BF)
    grads[...] = jnp.concatenate([grad_gate, grad_up, grad_low], axis=1)

    def product(cols):
        got = dot(hidden[...], down_v[:, cols]).astype(BF)
        back = dot(grads[...], weights[:, cols]).astype(BF)
        for o in range(2):
            base = o * (half + cap)
            outs[base : base + cap, cols] = got[o * cap : (o + 1) * cap, :]
            outs[base + cap : base + cap + half, cols] = back[o * half : (o + 1) * half, :]

    write_chunks(product, outs, mine, other, out_sems)
    second_o[0] = ADAPTER_SCALE * dot(low_v[:, :rank], grad_gate, TN)
    second_o[1] = ADAPTER_SCALE * dot(low_v[:, rank:], grad_up, TN)

    lanes = 2 * rank
    row = lax.broadcasted_iota(jnp.int32, (lanes, lanes), 0)
    col = lax.broadcasted_iota(jnp.int32, (lanes, lanes), 1)
    members = rank // 4
    away, factor, member = row // (2 * members), (row // members) % 2, row % members
    wanted = factor * rank + (place[2] ^ away) * members + member
    order = jnp.where(wanted == col, 1.0, 0.0).astype(BF)
    straight = place[1] == 0
    for k in range(N_Y):
        ours = grad_low[k * cap : (k + 1) * cap, :].astype(F32)
        theirs = grad_low[(N_Y + k) * cap : (N_Y + k + 1) * cap, :].astype(F32)
        rows = jnp.concatenate([jnp.where(straight, ours, theirs), jnp.where(straight, theirs, ours)], axis=0)
        at = pl.multiple_of(lax.div(block_of(place, k, False), 2) * 2 * cap, 2 * cap)
        low_t[:, pl.ds(at, 2 * cap)] = dot(order, rows.astype(BF), NT).astype(BF)
    finish_chunks(outs, mine, other, out_sems)
    wait(saved)


def rest(cap, place, near, far, pre_near, gate_up, down, first, second):
    width, h, both = down.shape[1], down.shape[0], 2 * second.shape[1]
    rows = 2 * N_Y * cap
    return call(
        functools.partial(rest_kernel, cap),
        [
            shape((both, rows)),
            shape((rows, width // (2 * N_Y))),
            shape(second.shape, F32),
            shape((rows // 2 + cap, width)),
            shape((rows // 2 + cap, width)),
        ],
        [place, *near, *far, *pre_near, gate_up, down, first, second],
        [SMEM] + [HBM] * 14 + [VMEM],
        [VMEM, HBM, VMEM, HBM, HBM],
        scratch=[
            pltpu.VMEM((2 * cap, width), BF),
            pltpu.VMEM((rows, width), BF),
            pltpu.VMEM((rows, h), F32),
            pltpu.VMEM((rows, h), F32),
            pltpu.VMEM((rows, both), BF),
            pltpu.VMEM((2 * h + both, width), BF),
            pltpu.VMEM(down.shape, BF),
            pltpu.VMEM((2 * cap, h), BF),
            pltpu.VMEM((rows, 2 * h + both), BF),
            pltpu.VMEM((rows + 2 * cap, width), BF),
            pltpu.SemaphoreType.DMA((8 * N_Y + 3,)),
            pltpu.SemaphoreType.DMA((8 + 2 * N_Y,)),
        ],
        flops=10**10,
        name="rest_rows",
    )


def pack_kernel(cap, n_z, place, *refs):
    sources, outs, (own, came, packed, sems, out_sems) = refs[:4], refs[4 : 4 + N_Y], refs[4 + N_Y :]
    n = N_Y
    core, x = place[1], place[2]
    lanes = own.shape[2] // (n_z * n)
    copies = []
    for which in range(2):
        for k in range(n):
            for i, target in enumerate((own, came)):
                near, last = sources[2 * i], sources[2 * i + 1]
                if which:
                    source = last.at[pl.ds((1 + k) * cap, cap), :]
                elif k == 2:
                    source = last.at[pl.ds(0, cap), :]
                else:
                    source = near.at[pl.ds(min(k, 2) * cap, cap), :]
                to = target.at[which, pl.ds(k * cap, cap), :]
                copies.append(start(source, to, sems.at[len(copies)]))

    def block(which, i, q, z):
        cols = pl.ds(pl.multiple_of(z * n * lanes + lax.rem(x + q, n) * lanes, lanes), lanes)
        here = own[which, i * cap : (i + 1) * cap, cols].astype(F32)
        j = (n - i) % n
        return (here + came[which, j * cap : (j + 1) * cap, cols].astype(F32)).astype(BF)

    def store(which, straight):
        for to in range(n):
            for slot in range(n):
                i, q = (to, slot) if straight else (slot, to)
                at = (2 * slot + which) * cap
                for z in range(n_z):
                    packed[to, at : at + cap, z * lanes : (z + 1) * lanes] = block(which, i, q, z)
            if which:
                start(packed.at[to], outs[to], out_sems.at[to])

    for which in range(2):
        wait(copies[which * 2 * n : (which + 1) * 2 * n])

        @pl.when(core == 0)
        def _():
            store(which, True)

        @pl.when(core == 1)
        def _():
            store(which, False)

    for to in range(n):
        pltpu.make_async_copy(packed.at[to], outs[to], out_sems.at[to]).wait()


def add_and_pack(cap, sources, place):
    n, n_z = N_Y, lax.axis_size("z")
    width = sources[0].shape[1]
    return call(
        functools.partial(pack_kernel, cap, n_z),
        [shape((2 * n * cap, width // n))] * n,
        [place, *sources],
        [SMEM] + [HBM] * len(sources),
        [HBM] * n,
        scratch=[pltpu.VMEM((2, n * cap, width), BF)] * 2
        + [
            pltpu.VMEM((n, 2 * n * cap, width // n), BF),
            pltpu.SemaphoreType.DMA((4 * n,)),
            pltpu.SemaphoreType.DMA((n,)),
        ],
        limit=20,
        name="add_and_pack",
    )


def total(parts):
    out = parts[0].astype(F32)
    for part in parts[1:]:
        out = out + part.astype(F32)
    return out


def first_moves(parts):
    return [parts[0]] + [crossed(parts[s], s, 0) for s in (2, 1, 3)]


def second_moves(once, n):
    cap = once.shape[0] // n
    blocks = [once[s * cap : (s + 1) * cap] for s in range(n)]
    return [blocks[0]] + [crossed(blocks[s], s, 1) for s in range(1, n)]


def to_tokens(rows, combine):
    n_z = lax.axis_size("z")
    cap = rows[0].shape[0]
    lanes = rows[0].shape[1] // n_z
    sent = [r.astype(BF).reshape(cap, n_z, lanes).transpose(1, 0, 2) for r in rows]
    came = lax.all_to_all(jnp.concatenate(sent, axis=2), "z", 0, 0, tiled=True)
    came = came.reshape(n_z * cap, len(rows) * lanes)
    sums = dot(combine, came).astype(BF)
    return [sums[:, i * lanes : (i + 1) * lanes] for i in range(len(rows))]


def shards(
    tokens,
    routed_experts,
    choice_weights,
    gate_up_weight,
    down_weight,
    adapter_first_factors,
    adapter_second_factors,
    cotangent,
):
    n_y, n_c, n_z, n_x = (lax.axis_size(a) for a in ("y", "core", "z", "x"))
    y, core, z, x = (lax.axis_index(a) for a in ("y", "core", "z", "x"))
    tok_count, width = tokens.shape
    cap = tok_count // 2
    rank = adapter_second_factors.shape[1]
    member_cols = rank // n_x
    hidden_count = down_weight.shape[0]
    part_width = width // (n_y * n_c)
    gate_up = gate_up_weight.swapaxes(1, 2).reshape(2 * hidden_count, width)

    place = jnp.stack([y, core, x, z]).astype(jnp.int32)
    own, far_first, row_gate = expert_rows(
        tokens, cotangent, adapter_first_factors, routed_experts.T, choice_weights.T, rank, place
    )
    chosen = jnp.any(routed_experts[:, :, None] == jnp.arange(n_z, dtype=jnp.int32), axis=1)
    earlier = jnp.arange(tok_count)[:, None] > jnp.arange(tok_count)[None, :]
    placed = dot(earlier.astype(BF), chosen.astype(BF)).astype(jnp.int32)
    combine = (placed[:, :, None] == jnp.arange(cap, dtype=jnp.int32)) & chosen[:, :, None]
    combine = combine.astype(BF).reshape(tok_count, n_z * cap)

    behind = ahead(own)
    front = ahead(own, -1)
    own_s = swap(own)
    far_first = ahead(far_first, 2)
    far_first_s = swap(far_first)
    behind, front, _ = lax.optimization_barrier((behind, front, far_first_s))
    front_s = swap(behind)
    behind_s = swap(front)
    far = ahead(tie(behind[own.shape[0] - 2 * cap :], front_s, behind_s))

    weights = (gate_up, down_weight)
    near = [own, front, behind, own_s, front_s, behind_s]
    *pre_near, mine_near, other_near, first = forward(
        cap, (0, 1, 3), place, near, [far_first, far_first_s], *weights, adapter_second_factors
    )
    came_near = swap(other_near)
    far = tie(far, mine_near)
    far_s = swap(far)
    low_t, x_part, second_gradient, mine_rest, other_rest = rest(
        cap, place, near, [far, far_s], pre_near, *weights, first, adapter_second_factors
    )

    def crossing(axis, bit):
        return [(i, i ^ bit) for i in range(lax.axis_size(axis))]

    cols = low_t.shape[0] // n_x
    low_sum = low_t.astype(F32) + swap(low_t).astype(F32)
    came_rest = swap(other_rest)
    sent = low_sum[2 * cols :].astype(BF)
    moved = lax.ppermute(sent, "x", crossing("x", 2))
    parts = add_and_pack(cap, [mine_near, mine_rest, came_near, came_rest], place)
    got = first_moves(parts)
    got_again = second_moves(total(got).astype(BF), n_y)
    pair = tie(low_sum[: 2 * cols], *got) + moved.astype(F32)
    sent = tie(pair[cols:].astype(BF), got_again[1])
    low_sum = pair[:cols] + lax.ppermute(sent, "x", crossing("x", 1)).astype(F32)
    low_sum = low_sum + lax.ppermute(low_sum, "y", crossing("y", 2))
    sums = total(got_again)
    mixed, token_gradient = to_tokens([sums[:cap] * row_gate, sums[cap:]], combine)
    summed = (low_sum + lax.ppermute(low_sum, "y", crossing("y", 1))).astype(BF)
    first_gradient = dot(summed, x_part).reshape(2, member_cols, part_width).transpose(0, 2, 1)
    return (mixed, token_gradient, first_gradient, second_gradient)


def solution(mesh):
    n_y, n_x = 4, 4
    n_dp, n_et = mesh.devices.shape
    fine = Mesh(
        mesh.devices.reshape(n_y, n_dp // n_y, n_et // n_x, n_x), ("y", "core", "z", "x")
    )
    dp, et = ("y", "core"), ("z", "x")
    both = et + dp
    return jax.shard_map(
        shards,
        mesh=fine,
        in_specs=(
            P(dp, None),
            P(dp, None),
            P(dp, None),
            P(None, None, both),
            P(both, None),
            P(None, dp, None),
            P(None, None, both),
            P(dp, None),
        ),
        out_specs=(P(dp, et), P(dp, et), P(None, dp, et), P(None, None, both)),
        check_vma=False,
    )
```
